128 devices in a mesh: wide: 16 (over z, y_lo, core), narrow: 8 (over y_hi, x).
Axes of the slice: x: 4, y: 4 (y_hi: 2, y_lo: 2; y = y_hi * 2 + y_lo), z: 4, core: 2. Of those that a mesh axis runs over, the one named last changes fastest.
Arguments:
- queries: bfloat16 [1024, 8192], P('wide', 'narrow'), may hold values from -12 to 12
- tenant: int32 [1024], replicated, may hold values from 0 to 31
- tenant_node_slot: int32 [32], replicated, may hold values from 0 to 31, each once
- suffix_length: int32 [1024], P('wide'), may hold values from 1 to 256, 131072 in all
- system_prompt_cache: bfloat16 [32768, 8, 256], P('wide', 'narrow'), may hold values from -9 to 9
- instruction_node_cache: bfloat16 [32, 2048, 8, 256], P('narrow', 'wide'), may hold values from -9 to 9
- suffix_cache: bfloat16 [1024, 256, 8, 256], P('wide', None, 'narrow'), may hold values from -400 to 400
- output_projection_weight: bfloat16 [8192, 5120], P('narrow'), may hold values from -0.5 to 0.5
- adapter_down_weight: bfloat16 [8192, 512], P('narrow'), may hold values from -0.5 to 0.5
- adapter_up_weight: bfloat16 [512, 5120], P(None, 'narrow'), may hold values from -1.5 to 1.5
Outputs:
- projected: bfloat16 [1024, 5120], P('wide', 'narrow')
The draws below stay inside these ranges and needn't reach their ends.
Inputs may be any that keep to these rules, and one draw needn't show every extreme that they name: `tenant_node_slot`: each of the 32 slots belongs to exactly one tenant. `suffix_length`: the longest suffix has exactly 256 positions.
All inputs are finite; a program needn't handle non-finite values. No bound on the sum of `suffix_length` on one device may be relied on, other than what follows from the above.
Results may differ from the reference program's by a relative error of at most 0.017.
Values may be sent and summed in bfloat16 or wider, within the bound.
No kernel may reach another device: no remote copies, remote signals or barrier semaphores. Data moves between devices by JAX's collectives and lax.ppermute only.
A program may use at most 320 MiB of HBM per device.

```python
import math
import jax
import jax.numpy as jnp
import numpy as np
from jax import lax

MODEL_WIDTH = 5120
QUERY_HEADS = 64
KVH = 8
HEAD_SIZE = 128
ADAPTER_RANK = 16
SUF = 256
ROWS = 1024
SYS = 32768
NODE = 2048
TENANT_COUNT = 32


def query_values(key):
    sample = jnp.clip(jax.random.normal(key, (ROWS, QUERY_HEADS * HEAD_SIZE), jnp.float32), -6.0, 6.0)
    return jnp.clip(sample, -12.0, 12.0)


def draw_queries(key, part):
    values = query_values(key)
    return values.astype(jnp.bfloat16)


def draw_suffix_cache(key, part):
    key = jax.random.fold_in(key, 7)
    sample = jnp.clip(jax.random.normal(key, (ROWS, SUF, KVH, 2 * HEAD_SIZE), jnp.float32), -6.0, 6.0) * 2.5
    sample = sample.at[:, :, :, HEAD_SIZE:].multiply(0.4)
    return sample.astype(jnp.bfloat16)


def with_ends(drawn, key, smallest, high):
    dims = drawn.shape
    index_at = [jax.random.randint(jax.random.fold_in(key, axis), (), 0, dims[axis]) for axis in range(len(dims))]
    drawn = drawn.at[tuple(index_at)].set(smallest)
    longest = dims.index(max(dims))
    index_at[longest] = (index_at[longest] + 1) % dims[longest]
    return drawn.at[tuple(index_at)].set(high)


def block_scale(stream_key, extent, pieces, least, top_value):
    loudness = 1.0
    for dim, blocks in pieces:
        heights = jax.random.uniform(jax.random.fold_in(jax.random.fold_in(stream_key, 6), dim), (blocks,), jnp.float32, least / len(pieces), top_value / len(pieces))
        loudness = loudness * jnp.repeat(jnp.exp(heights), extent[dim] // blocks).reshape((-1,) + (1,) * (len(extent) - 1 - dim))
    return loudness


def rank_bounds(amount, skew):
    portions = [(1 << 20) // math.isqrt(standing ** skew) + 1 for standing in range(1, amount + 1)]
    width = 1 + sum(portions) // (1 << 30)
    return np.cumsum(np.array([max(1, weight // width) for weight in portions]))


def skewed_ids(key, dims, count, lean):
    listing = rank_bounds(count, lean)
    pick = jax.random.randint(jax.random.fold_in(key, 1), dims, 0, int(listing[count - 1]))
    rank = jnp.searchsorted(jnp.asarray(listing, jnp.int32), pick, side="right")
    return jax.random.permutation(jax.random.fold_in(key, 2), count)[rank].astype(jnp.int32)


def split_up(count, total, most, skew):
    loads = [(1 << 20) // math.isqrt(grade ** skew) + 1 for grade in range(2, count + 1)]
    surplus, holding = total - most - (count - 1), [1] * (count - 1)
    while surplus > 0:
        candidates = [i for i in range(count - 1) if holding[i] < most]
        mass, remaining = sum([loads[i] for i in candidates]), surplus
        for i in candidates:
            extra = min(most - holding[i], max(1, remaining * loads[i] // mass), surplus)
            holding[i] = holding[i] + extra
            surplus = surplus - extra
    return np.array([most] + holding)


def uneven(rng, count, total, limit, skew):
    if count == 2:
        one = jax.random.randint(rng, (), max(1, total - limit), min(limit, total - 1) + 1)
        return jnp.stack([one, total - one])
    lengths = jnp.asarray(split_up(count, total, limit, skew), jnp.int32)
    couples = (count - 1) // 2
    source_of, taker = lengths[1:1 + 2 * couples:2], lengths[2:2 + 2 * couples:2]
    slack = jnp.minimum(source_of - 1, limit - taker)
    shifted = jax.random.randint(jax.random.fold_in(rng, 1), (couples,), 0, 1 << 20) % (slack + 1)
    lengths = lengths.at[1:1 + 2 * couples:2].set(source_of - shifted).at[2:2 + 2 * couples:2].set(taker + shifted)
    return lengths[jax.random.permutation(jax.random.fold_in(rng, 2), count)]


def scatter_about(stream_key, dims, width, bound, pieces=(), kind=jnp.bfloat16):
    values = width * jax.random.normal(stream_key, dims, jnp.float32)
    if pieces:
        values = values * block_scale(stream_key, dims, pieces, -0.22, 0.18)
    return jnp.clip(values, -bound, bound).astype(kind)


def setup_inputs(seed: int = 0) -> dict:
    key_of = jax.random.split(jax.random.key(seed), 11)
    queries = draw_queries(jax.random.fold_in(key_of[10], 71), 0)
    tenant = with_ends(skewed_ids(key_of[1], (ROWS,), TENANT_COUNT, 1), jax.random.fold_in(key_of[1], 3), 0, TENANT_COUNT - 1).astype(jnp.int32)
    tenant_node_slot = jax.random.permutation(key_of[2], TENANT_COUNT).astype(jnp.int32)
    suffix_length = uneven(key_of[3], ROWS, ROWS * SUF // 2, SUF, 2).astype(jnp.int32)
    system_prompt_cache = scatter_about(key_of[4], (SYS, KVH, 2 * HEAD_SIZE), 1.5, 9.0, ((0, 16), (1, 8)))
    instruction_node_cache = scatter_about(key_of[5], (TENANT_COUNT, NODE, KVH, 2 * HEAD_SIZE), 1.5, 9.0, ((0, 8), (1, 16)))
    suffix_cache = draw_suffix_cache(jax.random.fold_in(key_of[10], 71), 0)
    output_projection_weight = scatter_about(key_of[7], (QUERY_HEADS * HEAD_SIZE, MODEL_WIDTH), HEAD_SIZE ** -0.5, 0.5, ((0, 8),))
    adapter_down_weight = scatter_about(key_of[8], (QUERY_HEADS * HEAD_SIZE, TENANT_COUNT * ADAPTER_RANK), HEAD_SIZE ** -0.5, 0.5, ((0, 8),))
    adapter_up_weight = scatter_about(key_of[9], (TENANT_COUNT * ADAPTER_RANK, MODEL_WIDTH), ADAPTER_RANK ** -0.5, 1.5, ((1, 8),))
    return {"queries": queries, "tenant": tenant, "tenant_node_slot": tenant_node_slot, "suffix_length": suffix_length, "system_prompt_cache": system_prompt_cache, "instruction_node_cache": instruction_node_cache, "suffix_cache": suffix_cache, "output_projection_weight": output_projection_weight, "adapter_down_weight": adapter_down_weight, "adapter_up_weight": adapter_up_weight}


ADAPTER_SCALE = 1.0

def reference(queries, tenant, tenant_node_slot, suffix_length, system_prompt_cache, instruction_node_cache, suffix_cache, output_projection_weight, adapter_down_weight, adapter_up_weight):
    row_count = queries.shape[0]
    group_size = QUERY_HEADS // KVH
    inverse_sqrt_width = HEAD_SIZE ** (-0.5)
    suffix_span = suffix_cache.shape[1]
    row_slots = tenant_node_slot[tenant]
    block_rows = min(256, row_count)

    def one_head(kv_head):
        head_queries = lax.dynamic_slice_in_dim(queries, kv_head * group_size * HEAD_SIZE, group_size * HEAD_SIZE, 1)
        head_queries = head_queries.reshape(row_count, group_size, HEAD_SIZE).astype(jnp.float32)
        system_head = lax.dynamic_index_in_dim(system_prompt_cache, kv_head, 1, keepdims=False).astype(jnp.float32)
        node_head = lax.dynamic_index_in_dim(instruction_node_cache, kv_head, 2, keepdims=False)

        def one_block(offset):
            query_block = lax.dynamic_slice_in_dim(head_queries, offset, block_rows, 0)
            block_slots = lax.dynamic_slice_in_dim(row_slots, offset, block_rows, 0)
            block_lengths = lax.dynamic_slice_in_dim(suffix_length, offset, block_rows, 0)
            suffix_rows = lax.dynamic_slice_in_dim(suffix_cache, offset, block_rows, 0)
            suffix_head_state = lax.dynamic_index_in_dim(suffix_rows, kv_head, 2, keepdims=False).astype(jnp.float32)
            instruction_rows = jnp.take(node_head, block_slots, axis=0).astype(jnp.float32)
            system_scores = jnp.einsum('bgd,kd->bgk', query_block, system_head[:, :HEAD_SIZE]) * inverse_sqrt_width
            instruction_scores = jnp.einsum('ipn,izn->ipz', query_block, instruction_rows[:, :, :HEAD_SIZE]) * inverse_sqrt_width
            row_suffix_scores = jnp.einsum('ipn,izn->ipz', query_block, suffix_head_state[:, :, :HEAD_SIZE]) * inverse_sqrt_width
            in_suffix = (jnp.arange(suffix_span, dtype=jnp.int32)[None, :] < block_lengths[:, None])[:, None, :]
            row_suffix_scores = jnp.where(in_suffix, row_suffix_scores, -jnp.inf)
            highest = jnp.maximum(jnp.maximum(lax.optimization_barrier(jnp.max(system_scores, axis=2)), lax.optimization_barrier(jnp.max(instruction_scores, axis=2))), lax.optimization_barrier(jnp.max(row_suffix_scores, axis=2)))[..., None]
            system_weights = jnp.exp(system_scores - highest)
            node_weights = jnp.exp(instruction_scores - highest)
            suffix_weights = jnp.where(in_suffix, jnp.exp(row_suffix_scores - highest), 0.0)
            totals = lax.optimization_barrier(jnp.sum(system_weights, axis=2)) + lax.optimization_barrier(jnp.sum(node_weights, axis=2)) + lax.optimization_barrier(jnp.sum(suffix_weights, axis=2))
            rounded_values = (system_weights.astype(jnp.bfloat16), node_weights.astype(jnp.bfloat16), suffix_weights.astype(jnp.bfloat16))
            rounded_values = lax.optimization_barrier(rounded_values)
            weighted_values = jnp.einsum('bgk,kd->bgd', rounded_values[0].astype(jnp.float32), system_head[:, HEAD_SIZE:])
            weighted_values = weighted_values + jnp.einsum('vri,viu->vru', rounded_values[1].astype(jnp.float32), instruction_rows[:, :, HEAD_SIZE:])
            weighted_values = weighted_values + jnp.einsum('vri,viu->vru', rounded_values[2].astype(jnp.float32), suffix_head_state[:, :, HEAD_SIZE:])
            return (weighted_values / totals[..., None]).astype(jnp.bfloat16)
        offsets = jnp.arange(0, row_count, block_rows, dtype=jnp.int32)
        return lax.map(one_block, offsets).reshape(row_count, group_size * HEAD_SIZE)
    per_head = lax.map(one_head, jnp.arange(KVH, dtype=jnp.int32))
    attended_output = jnp.transpose(per_head, (1, 0, 2)).reshape(row_count, QUERY_HEADS * HEAD_SIZE)
    base_projection = jnp.dot(attended_output, output_projection_weight, preferred_element_type=jnp.float32)
    reduced_rank_state = jnp.dot(attended_output, adapter_down_weight, preferred_element_type=jnp.float32)
    tenant_of_column = jnp.arange(adapter_down_weight.shape[1], dtype=jnp.int32) // ADAPTER_RANK
    selected_adapter = jnp.where(tenant_of_column[None, :] == tenant[:, None], reduced_rank_state, 0.0).astype(jnp.bfloat16)
    adapter_delta = jnp.dot(selected_adapter, adapter_up_weight, preferred_element_type=jnp.float32)
    return (base_projection + ADAPTER_SCALE * adapter_delta).astype(jnp.bfloat16)
```

```python
import functools

import jax
import jax.numpy as jnp
from jax import lax
from jax.experimental import pallas as pl
from jax.experimental.pallas import tpu as pltpu
from jax.sharding import PartitionSpec as P

HEAD = 128
GROUP = 8
RANK = 16
F32 = jnp.float32
BF16 = jnp.bfloat16
SCALE2 = HEAD**-0.5 * 1.4426950408889634
FLOOR = -1e30
ROW_BLOCK = 256
KEY_BLOCK = 1024
VISIT_ROWS = 16
VISIT_UNROLL = 4
VMEM = 56 << 20


def _params():
    return pltpu.CompilerParams(
        vmem_limit_bytes=VMEM, dimension_semantics=("arbitrary",)
    )


def _lane(shape):
    return lax.broadcasted_iota(jnp.int32, shape, len(shape) - 1)


def _dot(a, b):
    return jnp.dot(a, b, preferred_element_type=F32)


def _system_kernel(q_ref, own_ref, sib_ref, o_ref, lse_ref, kt, ve):
    head = pl.program_id(0)
    n = own_ref.shape[0]

    @pl.when(head == 0)
    def _():
        for i, ref in enumerate((own_ref, sib_ref)):
            kt[:, i * n : (i + 1) * n] = ref[:, :HEAD].T
            ve[i * n : (i + 1) * n, :HEAD] = ref[:, HEAD:]
        ve[:, HEAD:] = jnp.ones((2 * n, HEAD), BF16)
        lse_ref[...] = jnp.zeros(lse_ref.shape, F32)

    rows = q_ref.shape[0]
    rb = min(ROW_BLOCK, rows)
    blocks = rows // rb
    lane = _lane((rb, HEAD))
    items = [(b, k) for b in range(blocks) for k in range(0, 2 * n, KEY_BLOCK)]

    def score(item):
        b, k = item
        return _dot(q_ref[b * rb : (b + 1) * rb, :], kt[:, k : k + KEY_BLOCK])

    top, total = [None] * blocks, [None] * blocks
    ahead = score(items[0])
    for i, (b, k) in enumerate(items):
        s = ahead
        if i + 1 < len(items):
            ahead = score(items[i + 1])
        high = jnp.max(s, axis=1, keepdims=True) * SCALE2
        if top[b] is not None:
            high = jnp.maximum(high, top[b])
        p = jnp.exp2(s * SCALE2 - high).astype(BF16)
        r = _dot(p, ve[k : k + KEY_BLOCK, :])
        if top[b] is None:
            total[b] = r
        else:
            total[b] = total[b] * jnp.exp2(top[b] - high) + r
        top[b] = high
    for b in range(blocks):
        l = total[b][:, HEAD:]
        at = slice(b * rb, (b + 1) * rb)
        o_ref[at, :] = total[b][:, :HEAD] / l
        lse = top[b] + jnp.log2(l)
        lse_ref[at, :] = jnp.where(lane == head, lse, lse_ref[at, :])


def _system(q, own, sib):
    rows, n = q.shape[0], own.shape[0]
    return pl.pallas_call(
        _system_kernel,
        grid=(GROUP,),
        in_specs=[
            pl.BlockSpec((rows, HEAD), lambda g: (0, g)),
            pl.BlockSpec((n, 2 * HEAD), lambda g: (0, 0)),
            pl.BlockSpec((n, 2 * HEAD), lambda g: (0, 0)),
        ],
        out_specs=[
            pl.BlockSpec((rows, HEAD), lambda g: (0, g)),
            pl.BlockSpec((rows, HEAD), lambda g: (0, 0)),
        ],
        out_shape=[
            jax.ShapeDtypeStruct((rows, GROUP * HEAD), F32),
            jax.ShapeDtypeStruct((rows, HEAD), F32),
        ],
        scratch_shapes=[
            pltpu.VMEM((HEAD, 2 * n), BF16),
            pltpu.VMEM((2 * n, 2 * HEAD), BF16),
        ],
        compiler_params=_params(),
        cost_estimate=pl.CostEstimate(
            flops=16 * rows * GROUP * n * HEAD,
            bytes_accessed=rows * 6 * GROUP * HEAD + 8 * n * HEAD,
            transcendentals=2 * rows * GROUP * n,
        ),
        name="system_attention",
    )(q, own, sib)


def _split3(x):
    hi = x.astype(BF16)
    rest = x - hi.astype(F32)
    mid = rest.astype(BF16)
    lo = (rest - mid.astype(F32)).astype(BF16)
    return hi.astype(F32), mid.astype(F32), lo.astype(F32)


def _pack3(x):
    lane = _lane(x.shape)
    hi, mid, lo = _split3(x)
    packed = jnp.where(lane < GROUP, hi, pltpu.roll(mid, GROUP, 1))
    packed = jnp.where(lane < 2 * GROUP, packed, pltpu.roll(lo, 2 * GROUP, 1))
    return jnp.where(lane < 3 * GROUP, packed, 0.0).astype(BF16)


def _unpack3(x):
    return x + (pltpu.roll(x, HEAD - GROUP, 1) + pltpu.roll(x, HEAD - 2 * GROUP, 1))


def _node_kernel(
    off_ref,
    slot_ref,
    q_ref,
    key_row_ref,
    key_col_ref,
    own_ref,
    sib_ref,
    o_sys_ref,
    lse_sys_ref,
    out_ref,
    qs,
    on,
    lse_n,
    visit_block,
    visit_tenant,
):
    rows = q_ref.shape[0]
    tenants = slot_ref.shape[0]
    vr = VISIT_ROWS

    def add_tenant(t, count):
        low, high = off_ref[t], off_ref[t + 1]
        first = low // vr
        last = jnp.where(high > low, (high + vr - 1) // vr, first)

        def add_block(b, c):
            visit_block[c] = b
            visit_tenant[c] = t
            return c + 1

        return lax.fori_loop(first, last, add_block, count)

    visits = lax.fori_loop(0, tenants, add_tenant, 0)
    for u in range(VISIT_UNROLL):
        visit_block[visits + u] = 0
        visit_tenant[visits + u] = tenants

    key_row, key_col = key_row_ref[...], key_col_ref[...]
    rank_row = jnp.sum((key_col < key_row).astype(jnp.int32), axis=0, keepdims=True)
    rank_col = jnp.sum((key_row < key_col).astype(jnp.int32), axis=1, keepdims=True)
    to_sorted = (
        lax.broadcasted_iota(jnp.int32, (rows, rows), 0) == rank_row
    ).astype(F32).astype(BF16)
    qs[...] = _dot(to_sorted, q_ref[...]).astype(BF16)

    lane = _lane((vr, HEAD))
    row_in_block = lax.broadcasted_iota(jnp.int32, (vr, HEAD), 0)

    def step(i, carry):
        blocks, spans, scores, slots = [], [], [], []
        for u in range(VISIT_UNROLL):
            v = i * VISIT_UNROLL + u
            b, t = visit_block[v], visit_tenant[v]
            slot = slot_ref[jnp.minimum(t, tenants - 1)]
            at = pl.ds(pl.multiple_of(b * vr, vr), vr)
            qb = jnp.concatenate(
                [qs[at, g * HEAD : (g + 1) * HEAD] for g in range(GROUP)], axis=0
            )
            dims = (((1,), (1,)), ((), ()))
            scores.append(
                [
                    lax.dot_general(
                        qb, ref[slot, :, :HEAD], dims, preferred_element_type=F32
                    )
                    for ref in (own_ref, sib_ref)
                ]
            )
            blocks.append(at)
            slots.append(slot)
            row = row_in_block + b * vr
            spans.append((row >= off_ref[t]) & (row < off_ref[t + 1]))
        tops, parts = [], []
        for s0, s1 in scores:
            high = jnp.max(jnp.maximum(s0, s1), axis=1, keepdims=True) * SCALE2
            p0 = jnp.exp2(s0 * SCALE2 - high)
            p1 = jnp.exp2(s1 * SCALE2 - high)
            tops.append(high)
            parts.append((p0, p1))
        results = []
        for (p0, p1), slot in zip(parts, slots):
            l = jnp.sum(p0 + p1, axis=1, keepdims=True)
            r = _dot(p0.astype(BF16), own_ref[slot, :, HEAD:]) + _dot(
                p1.astype(BF16), sib_ref[slot, :, HEAD:]
            )
            results.append((r, l))
        for at, inside, high, (r, l) in zip(blocks, spans, tops, results):
            o = r / l
            lse = high + jnp.log2(l)
            packed = jnp.zeros((vr, HEAD), F32)
            for g in range(GROUP):
                sub = slice(g * vr, (g + 1) * vr)
                cols = slice(g * HEAD, (g + 1) * HEAD)
                on[at, cols] = jnp.where(inside, o[sub, :], on[at, cols])
                packed = jnp.where(lane == g, lse[sub, :], packed)
            lse_n[at, :] = jnp.where(inside, packed, lse_n[at, :])
        return carry

    lax.fori_loop(0, (visits + VISIT_UNROLL - 1) // VISIT_UNROLL, step, 0)

    from_sorted = (
        lax.broadcasted_iota(jnp.int32, (rows, rows), 1) == rank_col
    ).astype(F32).astype(BF16)
    lse_node = _unpack3(_dot(from_sorted, _pack3(lse_n[...])))
    lse_sys = lse_sys_ref[...]
    top = jnp.maximum(lse_sys, lse_node)
    w_sys, w_node = jnp.exp2(lse_sys - top), jnp.exp2(lse_node - top)
    z = w_sys + w_node
    out_ref[:, GROUP * HEAD :] = _pack3(top + jnp.log2(z))
    w_sys, w_node = w_sys / z, w_node / z
    for g in range(GROUP):
        cols = slice(g * HEAD, (g + 1) * HEAD)
        o_node = _dot(from_sorted, on[:, cols].astype(BF16))
        out_ref[:, cols] = (
            w_sys[:, g : g + 1] * o_sys_ref[:, cols] + w_node[:, g : g + 1] * o_node
        ).astype(BF16)


def _node(off, slots, q, key, own, sib, o_sys, lse_sys):
    rows = q.shape[0]
    most = rows // VISIT_ROWS + slots.shape[0] + VISIT_UNROLL
    vmem = pl.BlockSpec(memory_space=pltpu.VMEM)
    return pl.pallas_call(
        _node_kernel,
        in_specs=[pl.BlockSpec(memory_space=pltpu.SMEM)] * 2 + [vmem] * 7,
        out_specs=vmem,
        out_shape=jax.ShapeDtypeStruct((rows, (GROUP + 1) * HEAD), BF16),
        scratch_shapes=[
            pltpu.VMEM((rows, GROUP * HEAD), BF16),
            pltpu.VMEM((rows, GROUP * HEAD), F32),
            pltpu.VMEM((rows, HEAD), F32),
            pltpu.SMEM((most,), jnp.int32),
            pltpu.SMEM((most,), jnp.int32),
        ],
        compiler_params=pltpu.CompilerParams(vmem_limit_bytes=VMEM),
        cost_estimate=pl.CostEstimate(
            flops=2 * 10**9, bytes_accessed=8 * 2**20, transcendentals=2**20
        ),
        name="node_attention",
    )(off, slots, q, key[None, :], key[:, None], own, sib, o_sys, lse_sys)


def _suffix_kernel(len_ref, q_ref, kv_ref, o_ref, lse_ref):
    rows, span = kv_ref.shape[0], kv_ref.shape[1]
    step = pl.program_id(0)
    position = _lane((GROUP, span))
    dims = (((1,), (1,)), ((), ()))
    scores = [
        lax.dot_general(
            q_ref[r], kv_ref[r, :, :HEAD], dims, preferred_element_type=F32
        )
        for r in range(rows)
    ]
    parts = []
    for r in range(rows):
        usable = position < len_ref[step * rows + r]
        s = jnp.where(usable, scores[r] * SCALE2, FLOOR)
        high = jnp.max(s, axis=1, keepdims=True)
        p = jnp.where(usable, jnp.exp2(s - high), 0.0)
        parts.append((p, high, jnp.sum(p, axis=1, keepdims=True)))
    for r in range(rows):
        p, high, l = parts[r]
        o_ref[r] = _dot(p.astype(BF16), kv_ref[r, :, HEAD:]) / l
        lse_ref[r] = jnp.broadcast_to(high + jnp.log2(l), (GROUP, HEAD))


def _suffix(lengths, q, kv):
    rows, span = kv.shape[0], kv.shape[1]
    block = 8
    shape = jax.ShapeDtypeStruct((rows, GROUP, HEAD), F32)
    spec = pl.BlockSpec((block, GROUP, HEAD), lambda i, n: (i, 0, 0))
    return pl.pallas_call(
        _suffix_kernel,
        grid_spec=pltpu.PrefetchScalarGridSpec(
            num_scalar_prefetch=1,
            grid=(rows // block,),
            in_specs=[
                spec,
                pl.BlockSpec((block, span, 2 * HEAD), lambda i, n: (i, 0, 0)),
            ],
            out_specs=[spec, spec],
        ),
        out_shape=[shape, shape],
        compiler_params=_params(),
        cost_estimate=pl.CostEstimate(
            flops=10**9, bytes_accessed=rows * span * 512, transcendentals=2**17
        ),
        name="suffix_attention",
    )(lengths, q.reshape(rows, GROUP, HEAD), kv)


def _project_kernel(
    tenant_ref, recv_ref, o_ref, lse_ref, w_ref, down_ref, out_ref, att, low
):
    parts, rows = recv_ref.shape[0], recv_ref.shape[1]

    @pl.when(pl.program_id(0) == 0)
    def _():
        lane = _lane((rows, HEAD))
        own = jnp.zeros((rows, HEAD), F32)
        for g in range(GROUP):
            own = jnp.where(lane == g, lse_ref[:, g, :], own)
        lses = [own] + [
            _unpack3(recv_ref[w, :, GROUP * HEAD :].astype(F32)) for w in range(parts)
        ]
        top = functools.reduce(jnp.maximum, lses)
        weights = [jnp.exp2(x - top) for x in lses]
        z = functools.reduce(jnp.add, weights)
        weights = [x / z for x in weights]
        for g in range(GROUP):
            cols = slice(g * HEAD, (g + 1) * HEAD)
            acc = weights[0][:, g : g + 1] * o_ref[:, g, :]
            for w in range(parts):
                acc += weights[1 + w][:, g : g + 1] * recv_ref[w, :, cols].astype(F32)
            att[:, cols] = acc.astype(BF16)
        reduced = _dot(att[...], down_ref[...])
        width = reduced.shape[1]
        mine = _lane((rows, width)) // RANK == tenant_ref[...]
        reduced = jnp.where(mine, reduced, 0.0)
        kept = reduced[:, :HEAD]
        for c in range(HEAD, width, HEAD):
            kept = kept + reduced[:, c : c + HEAD]
        low[...] = kept.astype(BF16)

    width = w_ref.shape[1]
    out_ref[0, :, :width] = _dot(att[...], w_ref[...]).astype(BF16)
    out_ref[0, :, width:] = low[...]


def _project(tenant, recv, o, lse, weight, down, parts):
    rows = recv.shape[1]
    depth, features = weight.shape
    width = features // parts

    def whole(shape):
        return pl.BlockSpec(shape, lambda d: (0,) * len(shape))

    return pl.pallas_call(
        _project_kernel,
        grid=(parts,),
        in_specs=[
            whole((rows, 1)),
            whole(recv.shape),
            whole(o.shape),
            whole(lse.shape),
            pl.BlockSpec((depth, width), lambda d: (0, d)),
            whole(down.shape),
        ],
        out_specs=pl.BlockSpec((1, rows, width + HEAD), lambda d: (d, 0, 0)),
        out_shape=jax.ShapeDtypeStruct((parts, rows, width + HEAD), BF16),
        scratch_shapes=[
            pltpu.VMEM((rows, GROUP * HEAD), BF16),
            pltpu.VMEM((rows, HEAD), BF16),
        ],
        compiler_params=_params(),
        cost_estimate=pl.CostEstimate(
            flops=2 * rows * depth * features,
            bytes_accessed=2 * depth * features,
            transcendentals=0,
        ),
        name="project",
    )(tenant, recv, o, lse, weight, down)


def _finish_kernel(tenant_ref, recv_ref, up_ref, out_ref):
    parts, rows = recv_ref.shape[0], recv_ref.shape[1]
    width = out_ref.shape[1]
    total = recv_ref[0].astype(F32)
    for w in range(1, parts):
        total += recv_ref[w].astype(F32)
    depth = up_ref.shape[0]
    low = jnp.concatenate([total[:, width:]] * (depth // HEAD), axis=1)
    mine = _lane((rows, depth)) // RANK == tenant_ref[...]
    chosen = jnp.where(mine, low, 0.0).astype(BF16)
    out_ref[...] = (total[:, :width] + _dot(chosen, up_ref[...])).astype(BF16)


def _finish(tenant, recv, up):
    vmem = pl.BlockSpec(memory_space=pltpu.VMEM)
    return pl.pallas_call(
        _finish_kernel,
        in_specs=[vmem] * 3,
        out_specs=vmem,
        out_shape=jax.ShapeDtypeStruct((recv.shape[1], up.shape[1]), BF16),
        compiler_params=pltpu.CompilerParams(vmem_limit_bytes=VMEM),
        name="finish",
    )(tenant, recv, up)


def per_device(
    queries,
    tenant,
    tenant_node_slot,
    suffix_length,
    system_prompt_cache,
    instruction_node_cache,
    suffix_cache,
    output_projection_weight,
    adapter_down_weight,
    adapter_up_weight,
):
    rows, width = queries.shape
    n_wide = lax.axis_size("wide")
    n_narrow = lax.axis_size("narrow")
    chips = n_wide // 2
    position = lax.axis_index("wide")
    core = position % 2
    same_core = [[2 * j + c for j in range(chips)] for c in range(2)]
    sibling = [(i, i ^ 1) for i in range(n_wide)]
    n_slots = tenant_node_slot.shape[0]
    span = instruction_node_cache.shape[1]

    q = lax.all_to_all(
        jnp.broadcast_to(queries[None], (chips, rows, width)),
        "wide",
        0,
        0,
        axis_index_groups=same_core,
        tiled=True,
    ).reshape(chips * rows, width)

    own = system_prompt_cache.reshape(-1, 2 * HEAD)
    sib = lax.ppermute(own, "wide", sibling)

    by_head = jnp.transpose(instruction_node_cache, (2, 0, 1, 3))
    q, by_head = lax.optimization_barrier((q, by_head))
    nodes = lax.all_to_all(by_head, "narrow", 0, 0, tiled=True)
    nodes = nodes.reshape(n_slots, span, 2 * HEAD)
    nodes_sib = lax.ppermute(nodes, "wide", sibling)

    by_core = tenant.reshape(chips, 2, rows)
    mine = jnp.where(core == 0, by_core[:, 0], by_core[:, 1]).reshape(-1)
    key = mine * (chips * rows) + jnp.arange(chips * rows, dtype=jnp.int32)
    bounds = jnp.arange(n_slots + 2, dtype=jnp.int32)
    off = jnp.sum((mine[None, :] < bounds[:, None]).astype(jnp.int32), axis=1)

    o_suf, lse_suf = _suffix(
        suffix_length, queries, suffix_cache.reshape(rows, -1, 2 * HEAD)
    )
    o_sys, lse_sys = _system(q, own, sib)
    sent = _node(off, tenant_node_slot, q, key, nodes, nodes_sib, o_sys, lse_sys)
    recv = lax.all_to_all(
        sent.reshape(chips, rows, -1),
        "wide",
        0,
        0,
        axis_index_groups=same_core,
        tiled=True,
    )
    my_tenant = lax.dynamic_slice_in_dim(tenant, position * rows, rows, 0)[:, None]
    parts = _project(
        my_tenant,
        recv,
        o_suf,
        lse_suf,
        output_projection_weight,
        adapter_down_weight,
        n_narrow,
    )
    parts = lax.all_to_all(parts, "narrow", 0, 0, tiled=True)
    return _finish(my_tenant, parts, adapter_up_weight)


def solution(mesh):
    return jax.shard_map(
        per_device,
        mesh=mesh,
        in_specs=(
            P("wide", "narrow"),
            P(),
            P(),
            P("wide"),
            P("wide", "narrow", None),
            P("narrow", "wide", None, None),
            P("wide", None, "narrow", None),
            P("narrow", None),
            P("narrow", None),
            P(None, "narrow"),
        ),
        out_specs=P("wide", "narrow"),
        check_vma=False,
    )
```

```python
import functools

import jax
import jax.numpy as jnp
from jax import lax
from jax.experimental import pallas as pl
from jax.experimental.pallas import tpu as pltpu
from jax.sharding import PartitionSpec as P

HEAD = 128
GROUP = 8
RANK = 16
F32 = jnp.float32
BF16 = jnp.bfloat16
SCALE2 = HEAD**-0.5 * 1.4426950408889634
FLOOR = -1e30
KEY_BLOCK = 2048
HEADS_AT_ONCE = 2
VISIT_ROWS = 16
VISIT_UNROLL = 8


def _params(mib, grid=True):
    return pltpu.CompilerParams(
        vmem_limit_bytes=mib << 20,
        dimension_semantics=("arbitrary",) if grid else None,
    )


def _in_hbm(x):
    return pltpu.with_memory_space_constraint(x, pltpu.HBM)


def _lane(shape):
    return lax.broadcasted_iota(jnp.int32, shape, len(shape) - 1)


def _dot(a, b):
    return jnp.dot(a, b, preferred_element_type=F32)


def _keys_kernel(own_ref, sib_ref, kt_ref, ve_ref):
    n = own_ref.shape[0]
    for i, ref in enumerate((own_ref, sib_ref)):
        at = slice(i * n, (i + 1) * n)
        kt_ref[:, at] = ref[:, :HEAD].T
        ve_ref[at, :HEAD] = ref[:, HEAD:]
        ve_ref[at, HEAD:] = jnp.ones((n, HEAD), BF16)


def _keys(own, sib):
    n = 2 * own.shape[0]
    vmem = pl.BlockSpec(memory_space=pltpu.VMEM)
    return pl.pallas_call(
        _keys_kernel,
        in_specs=[vmem] * 2,
        out_specs=[vmem] * 2,
        out_shape=[
            jax.ShapeDtypeStruct((HEAD, n), BF16),
            jax.ShapeDtypeStruct((n, 2 * HEAD), BF16),
        ],
        compiler_params=_params(16, False),
        cost_estimate=pl.CostEstimate(
            flops=0, bytes_accessed=10 * n * HEAD, transcendentals=0
        ),
        name="keys",
    )(own, sib)


def _system_kernel(count, *refs):
    q_refs, (kt, ve) = refs[:count], refs[count : count + 2]
    o_refs, lse_refs = refs[count + 2 : 2 * count + 2], refs[2 * count + 2 :]
    step = pl.program_id(0)
    rows, keys = q_refs[0].shape[0], kt.shape[1]
    lane = _lane((rows, HEAD))
    items = [
        (h, b, k)
        for h in range(HEADS_AT_ONCE)
        for b in range(count)
        for k in range(0, keys, KEY_BLOCK)
    ]

    def score(item):
        h, b, k = item
        q = q_refs[b][:, h * HEAD : (h + 1) * HEAD]
        return _dot(q, kt[:, k : k + KEY_BLOCK])

    top, total = {}, {}
    ahead = score(items[0])
    for i, (h, b, k) in enumerate(items):
        s = ahead
        if i + 1 < len(items):
            ahead = score(items[i + 1])
        high = jnp.max(s, axis=1, keepdims=True) * SCALE2
        if (h, b) in top:
            high = jnp.maximum(high, top[h, b])
        p = jnp.exp2(s * SCALE2 - high).astype(BF16)
        r = _dot(p, ve[k : k + KEY_BLOCK, :])
        if (h, b) in top:
            r = total[h, b] * jnp.exp2(top[h, b] - high) + r
        top[h, b], total[h, b] = high, r
    for b in range(count):
        packed = jnp.where(step == 0, 0.0, lse_refs[b][...])
        for h in range(HEADS_AT_ONCE):
            l = total[h, b][:, HEAD:]
            o_refs[b][:, h * HEAD : (h + 1) * HEAD] = total[h, b][:, :HEAD] / l
            lse = top[h, b] + jnp.log2(l)
            packed = jnp.where(lane == step * HEADS_AT_ONCE + h, lse, packed)
        lse_refs[b][...] = packed


def _system(qs, kt, ve):
    count, rows, keys = len(qs), qs[0].shape[0], ve.shape[0]
    heads = pl.BlockSpec((rows, HEADS_AT_ONCE * HEAD), lambda g: (0, g))
    fixed = pl.BlockSpec((rows, HEAD), lambda g: (0, 0))
    outs = pl.pallas_call(
        functools.partial(_system_kernel, count),
        grid=(GROUP // HEADS_AT_ONCE,),
        in_specs=[heads] * count
        + [
            pl.BlockSpec(kt.shape, lambda g: (0, 0)),
            pl.BlockSpec(ve.shape, lambda g: (0, 0)),
        ],
        out_specs=[heads] * count + [fixed] * count,
        out_shape=[pltpu.HBM((rows, GROUP * HEAD), F32)] * count
        + [pltpu.HBM((rows, HEAD), F32)] * count,
        compiler_params=_params(32),
        cost_estimate=pl.CostEstimate(
            flops=6 * count * rows * GROUP * keys * HEAD,
            bytes_accessed=count * rows * 6 * GROUP * HEAD + 6 * keys * HEAD,
            transcendentals=count * rows * GROUP * keys,
        ),
        name="system_attention",
    )(*qs, kt, ve)
    return list(outs[:count]), list(outs[count:])


def _split3(x):
    hi = x.astype(BF16)
    rest = x - hi.astype(F32)
    mid = rest.astype(BF16)
    lo = (rest - mid.astype(F32)).astype(BF16)
    return hi.astype(F32), mid.astype(F32), lo.astype(F32)


def _pack3(x):
    lane = _lane(x.shape)
    hi, mid, lo = _split3(x)
    packed = jnp.where(lane < GROUP, hi, pltpu.roll(mid, GROUP, 1))
    packed = jnp.where(lane < 2 * GROUP, packed, pltpu.roll(lo, 2 * GROUP, 1))
    return jnp.where(lane < 3 * GROUP, packed, 0.0).astype(BF16)


def _unpack3(x):
    return x + (pltpu.roll(x, HEAD - GROUP, 1) + pltpu.roll(x, HEAD - 2 * GROUP, 1))


def _plan_kernel(slot_ref, row_ref, col_ref, *refs):
    q_refs, (qs_ref, back_ref, table_ref) = refs[:-3], refs[-3:]
    rows = qs_ref.shape[0]
    piece = q_refs[0].shape[0]
    tenants = slot_ref.shape[0]
    width = table_ref.shape[1]
    t_row, t_col = row_ref[...], col_ref[...]

    def iota(shape, dim):
        return lax.broadcasted_iota(jnp.int32, shape, dim)

    def count(where, axis):
        return jnp.sum(where.astype(jnp.int32), axis=axis, keepdims=True)

    key_row = t_row * rows + iota((1, rows), 1)
    key_col = t_col * rows + iota((rows, 1), 0)
    rank_row = count(key_col < key_row, 0)
    rank_col = count(key_row < key_col, 1)
    to_sorted = (iota((rows, rows), 0) == rank_row).astype(F32).astype(BF16)
    back_ref[...] = (iota((rows, rows), 1) == rank_col).astype(F32).astype(BF16)
    qs_ref[...] = sum(
        _dot(to_sorted[:, i * piece : (i + 1) * piece], ref[...])
        for i, ref in enumerate(q_refs)
    ).astype(BF16)

    def visits_of(low, high):
        first = low // VISIT_ROWS
        last = (high + VISIT_ROWS - 1) // VISIT_ROWS
        return first, jnp.where(high > low, last - first, 0)

    lane = iota((1, width), 1)
    _, n_row = visits_of(count(t_col < lane, 0), count(t_col < lane + 1, 0))
    t = iota((tenants, 1), 0)
    low, high = count(t_row < t, 1), count(t_row < t + 1, 1)
    first, n = visits_of(low, high)
    start = jnp.sum(jnp.where(lane < t, n_row, 0), axis=1, keepdims=True)
    here = (lane >= start) & (lane < start + n)

    def pick(column):
        return jnp.sum(jnp.where(here, column, 0), axis=0, keepdims=True)

    table_ref[...] = jnp.concatenate(
        [
            pick(first - start + lane),
            pick(slot_ref[...]),
            pick(low),
            pick(high),
            jnp.broadcast_to(jnp.sum(n, axis=0, keepdims=True), (1, width)),
        ]
        + [jnp.zeros((1, width), jnp.int32)] * 3,
        axis=0,
    )


def _plan(slots, mine, qs):
    rows, width = mine.shape[0], qs[0].shape[1]
    vmem = pl.BlockSpec(memory_space=pltpu.VMEM)
    return pl.pallas_call(
        _plan_kernel,
        in_specs=[vmem] * (3 + len(qs)),
        out_specs=[vmem] * 3,
        out_shape=[
            jax.ShapeDtypeStruct((rows, width), BF16),
            jax.ShapeDtypeStruct((rows, rows), BF16),
            jax.ShapeDtypeStruct((8, HEAD), jnp.int32),
        ],
        compiler_params=_params(16, False),
        cost_estimate=pl.CostEstimate(
            flops=2 * rows * rows * width,
            bytes_accessed=6 * rows * width,
            transcendentals=0,
        ),
        name="plan",
    )(slots[:, None], mine[None, :], mine[:, None], *qs)


def _node_kernel(count, table, order, qs, back_ref, own_ref, sib_ref, *refs):
    o_hbm, lse_hbm = refs[:count], refs[count : 2 * count]
    out_ref, on, lse_n, o_buf, lse_buf, sems = refs[2 * count :]
    fetches = [
        pltpu.make_async_copy(src, dst, sems.at[i])
        for i, (src, dst) in enumerate(
            [(o_hbm[i], o_buf.at[i]) for i in range(count)]
            + [(lse_hbm[i], lse_buf.at[i]) for i in range(count)]
        )
    ]
    for fetch in fetches:
        fetch.start()
    vr = VISIT_ROWS
    lane = _lane((vr, HEAD))
    row_in_block = lax.broadcasted_iota(jnp.int32, (vr, HEAD), 0)
    dims = (((1,), (1,)), ((), ()))

    def step(i, carry):
        blocks, spans, scores, slots = [], [], [], []
        for u in range(VISIT_UNROLL):
            v = i * VISIT_UNROLL + u
            at = pl.ds(pl.multiple_of(table[0, v] * vr, vr), vr)
            slot = table[1, v]
            qb = jnp.concatenate(
                [qs[at, g * HEAD : (g + 1) * HEAD] for g in range(GROUP)], axis=0
            )
            scores.append(
                [
                    lax.dot_general(
                        qb, ref[slot, :, :HEAD], dims, preferred_element_type=F32
                    )
                    for ref in (own_ref, sib_ref)
                ]
            )
            blocks.append(at)
            slots.append(slot)
            row = row_in_block + table[0, v] * vr
            spans.append((row >= table[2, v]) & (row < table[3, v]))
        tops, parts = [], []
        for s0, s1 in scores:
            high = jnp.max(jnp.maximum(s0, s1), axis=1, keepdims=True) * SCALE2
            p0 = jnp.exp2(s0 * SCALE2 - high)
            p1 = jnp.exp2(s1 * SCALE2 - high)
            tops.append(high)
            parts.append((p0, p1))
        results = []
        for (p0, p1), slot in zip(parts, slots):
            l = jnp.sum(p0 + p1, axis=1, keepdims=True)
            r = _dot(p0.astype(BF16), own_ref[slot, :, HEAD:]) + _dot(
                p1.astype(BF16), sib_ref[slot, :, HEAD:]
            )
            results.append((r, l))
        for at, inside, high, (r, l) in zip(blocks, spans, tops, results):
            o = r / l
            lse = high + jnp.log2(l)
            packed = jnp.zeros((vr, HEAD), F32)
            for g in range(GROUP):
                sub = slice(g * vr, (g + 1) * vr)
                cols = slice(g * HEAD, (g + 1) * HEAD)
                on[at, cols] = jnp.where(inside, o[sub, :], on[at, cols].astype(F32)).astype(
                    BF16
                )
                packed = jnp.where(lane == g, lse[sub, :], packed)
            lse_n[at, :] = jnp.where(inside, packed, lse_n[at, :])
        return carry

    lax.fori_loop(0, (table[4, 0] + VISIT_UNROLL - 1) // VISIT_UNROLL, step, 0)

    for fetch in fetches:
        fetch.wait()
    packed_lse = _pack3(lse_n[...])
    piece = o_buf.shape[1]
    for i in range(count):
        back = back_ref[i * piece : (i + 1) * piece, :]
        to = pl.ds(pl.multiple_of(order[i] * piece, piece), piece)
        lse_node = _unpack3(_dot(back, packed_lse))
        lse_sys = lse_buf[i]
        top = jnp.maximum(lse_sys, lse_node)
        w_sys, w_node = jnp.exp2(lse_sys - top), jnp.exp2(lse_node - top)
        z = w_sys + w_node
        out_ref[to, GROUP * HEAD :] = _pack3(top + jnp.log2(z))
        w_sys, w_node = w_sys / z, w_node / z
        for g in range(GROUP):
            cols = slice(g * HEAD, (g + 1) * HEAD)
            o_node = _dot(back, on[:, cols])
            out_ref[to, cols] = (
                w_sys[:, g : g + 1] * o_buf[i, :, cols]
                + w_node[:, g : g + 1] * o_node
            ).astype(BF16)


def _node(table, order, qs, back, own, sib, o_sys, lse_sys):
    rows, count = qs.shape[0], len(o_sys)
    smem = pl.BlockSpec(memory_space=pltpu.SMEM)
    hbm = pl.BlockSpec(memory_space=pltpu.HBM)
    piece = o_sys[0].shape[0]
    vmem = pl.BlockSpec(memory_space=pltpu.VMEM)
    return pl.pallas_call(
        functools.partial(_node_kernel, count),
        in_specs=[smem] * 2 + [vmem] * 4 + [hbm] * (2 * count),
        out_specs=vmem,
        out_shape=jax.ShapeDtypeStruct((rows, (GROUP + 1) * HEAD), BF16),
        scratch_shapes=[
            pltpu.VMEM((rows, GROUP * HEAD), BF16),
            pltpu.VMEM((rows, HEAD), F32),
            pltpu.VMEM((count, piece, GROUP * HEAD), F32),
            pltpu.VMEM((count, piece, HEAD), F32),
            pltpu.SemaphoreType.DMA((2 * count,)),
        ],
        compiler_params=_params(24, False),
        cost_estimate=pl.CostEstimate(
            flops=2 * 10**9, bytes_accessed=8 * 2**20, transcendentals=2**20
        ),
        name="node_attention",
    )(table, order, qs, back, own, sib, *map(_in_hbm, [*o_sys, *lse_sys]))


def _suffix_kernel(len_ref, q_ref, kv_hbm, o_ref, lse_ref, kv_ref, sems):
    rows, span = kv_ref.shape[0], kv_ref.shape[1]
    block = rows // sems.shape[0]
    fetches = [
        pltpu.make_async_copy(
            kv_hbm.at[pl.ds(i * block, block)],
            kv_ref.at[pl.ds(i * block, block)],
            sems.at[i],
        )
        for i in range(sems.shape[0])
    ]
    for fetch in fetches:
        fetch.start()
    position = _lane((GROUP, span))
    dims = (((1,), (1,)), ((), ()))
    for i, fetch in enumerate(fetches):
        fetch.wait()
        here = range(i * block, (i + 1) * block)
        scores = [
            lax.dot_general(
                q_ref[r], kv_ref[r, :, :HEAD], dims, preferred_element_type=F32
            )
            for r in here
        ]
        parts = []
        for r, s in zip(here, scores):
            usable = position < len_ref[r]
            s = jnp.where(usable, s * SCALE2, FLOOR)
            high = jnp.max(s, axis=1, keepdims=True)
            p = jnp.where(usable, jnp.exp2(s - high), 0.0)
            parts.append((p, high, jnp.sum(p, axis=1, keepdims=True)))
        for r, (p, high, l) in zip(here, parts):
            o_ref[r] = _dot(p.astype(BF16), kv_ref[r, :, HEAD:]) / l
            lse_ref[r] = jnp.broadcast_to(high + jnp.log2(l), (GROUP, HEAD))


def _suffix(lengths, q, kv):
    rows, span = kv.shape[0], kv.shape[1]
    shape = jax.ShapeDtypeStruct((rows, GROUP, HEAD), F32)
    vmem = pl.BlockSpec(memory_space=pltpu.VMEM)
    return pl.pallas_call(
        _suffix_kernel,
        in_specs=[
            pl.BlockSpec(memory_space=pltpu.SMEM),
            vmem,
            pl.BlockSpec(memory_space=pltpu.HBM),
        ],
        out_specs=[vmem, vmem],
        out_shape=[shape, shape],
        scratch_shapes=[
            pltpu.VMEM(kv.shape, BF16),
            pltpu.SemaphoreType.DMA((8,)),
        ],
        compiler_params=_params(24, False),
        cost_estimate=pl.CostEstimate(
            flops=10**9, bytes_accessed=rows * span * 512, transcendentals=2**17
        ),
        name="suffix_attention",
    )(lengths, q.reshape(rows, GROUP, HEAD), _in_hbm(kv))


def _project_kernel(
    tenant_ref,
    recv_ref,
    o_ref,
    lse_ref,
    w_hbm,
    down_hbm,
    out_ref,
    att,
    low,
    w_ref,
    down_ref,
    sems,
):
    parts, rows = recv_ref.shape[0], recv_ref.shape[1]
    step = pl.program_id(0)
    width = w_ref.shape[2]

    def fetch_w(d):
        at = pl.multiple_of(d * width, HEAD)
        return pltpu.make_async_copy(
            w_hbm.at[:, pl.ds(at, width)], w_ref.at[d], sems.at[d]
        )

    fetch_down = pltpu.make_async_copy(down_hbm, down_ref, sems.at[w_ref.shape[0]])

    @pl.when(step == 0)
    def _():
        fetch_down.start()
        for d in range(w_ref.shape[0]):
            fetch_w(d).start()
        lane = _lane((rows, HEAD))
        own = jnp.zeros((rows, HEAD), F32)
        for g in range(GROUP):
            own = jnp.where(lane == g, lse_ref[:, g, :], own)
        lses = [own] + [
            _unpack3(recv_ref[w, :, GROUP * HEAD :].astype(F32)) for w in range(parts)
        ]
        top = functools.reduce(jnp.maximum, lses)
        weights = [jnp.exp2(x - top) for x in lses]
        z = functools.reduce(jnp.add, weights)
        weights = [x / z for x in weights]
        for g in range(GROUP):
            cols = slice(g * HEAD, (g + 1) * HEAD)
            acc = weights[0][:, g : g + 1] * o_ref[:, g, :]
            for w in range(parts):
                acc += weights[1 + w][:, g : g + 1] * recv_ref[w, :, cols].astype(F32)
            att[:, cols] = acc.astype(BF16)
        fetch_down.wait()
        reduced = _dot(att[...], down_ref[...])
        mine = _lane(reduced.shape) // RANK == tenant_ref[...]
        reduced = jnp.where(mine, reduced, 0.0)
        kept = reduced[:, :HEAD]
        for c in range(HEAD, reduced.shape[1], HEAD):
            kept = kept + reduced[:, c : c + HEAD]
        low[...] = kept.astype(BF16)

    fetch_w(step).wait()
    out_ref[0, :, :width] = _dot(att[...], w_ref[step]).astype(BF16)
    out_ref[0, :, width:] = low[...]


def _project(tenant, recv, o, lse, weight, down, parts):
    rows = recv.shape[1]
    depth, features = weight.shape
    width = features // parts

    def whole(shape):
        return pl.BlockSpec(shape, lambda d: (0,) * len(shape))

    return pl.pallas_call(
        _project_kernel,
        grid=(parts,),
        in_specs=[
            whole((rows, 1)),
            whole(recv.shape),
            whole(o.shape),
            whole(lse.shape),
            pl.BlockSpec(memory_space=pltpu.HBM),
            pl.BlockSpec(memory_space=pltpu.HBM),
        ],
        out_specs=pl.BlockSpec((1, rows, width + HEAD), lambda d: (d, 0, 0)),
        out_shape=jax.ShapeDtypeStruct((parts, rows, width + HEAD), BF16),
        scratch_shapes=[
            pltpu.VMEM((rows, GROUP * HEAD), BF16),
            pltpu.VMEM((rows, HEAD), BF16),
            pltpu.VMEM((parts, depth, width), BF16),
            pltpu.VMEM(down.shape, BF16),
            pltpu.SemaphoreType.DMA((parts + 1,)),
        ],
        compiler_params=_params(32),
        cost_estimate=pl.CostEstimate(
            flops=2 * rows * depth * features,
            bytes_accessed=2 * depth * features,
            transcendentals=0,
        ),
        name="project",
    )(tenant, recv, o, lse, _in_hbm(weight), _in_hbm(down))


def _finish_kernel(tenant_ref, recv_ref, up_ref, out_ref):
    parts, rows = recv_ref.shape[0], recv_ref.shape[1]
    width = out_ref.shape[1]
    total = recv_ref[0].astype(F32)
    for w in range(1, parts):
        total += recv_ref[w].astype(F32)
    depth = up_ref.shape[0]
    low = jnp.concatenate([total[:, width:]] * (depth // HEAD), axis=1)
    mine = _lane((rows, depth)) // RANK == tenant_ref[...]
    chosen = jnp.where(mine, low, 0.0).astype(BF16)
    out_ref[...] = (total[:, :width] + _dot(chosen, up_ref[...])).astype(BF16)


def _finish(tenant, recv, up):
    vmem = pl.BlockSpec(memory_space=pltpu.VMEM)
    return pl.pallas_call(
        _finish_kernel,
        in_specs=[vmem] * 3,
        out_specs=vmem,
        out_shape=jax.ShapeDtypeStruct((recv.shape[1], up.shape[1]), BF16),
        compiler_params=_params(16, False),
        name="finish",
    )(tenant, recv, up)


def per_device(
    queries,
    tenant,
    tenant_node_slot,
    suffix_length,
    system_prompt_cache,
    instruction_node_cache,
    suffix_cache,
    output_projection_weight,
    adapter_down_weight,
    adapter_up_weight,
):
    rows, width = queries.shape
    n_wide = lax.axis_size("wide")
    n_narrow = lax.axis_size("narrow")
    chips = n_wide // 2
    layers = chips // 2
    position = lax.axis_index("wide")
    layer, side, core = position // 4, position // 2 % 2, position % 2
    same_core = [[2 * j + c for j in range(chips)] for c in range(2)]
    sibling = [(i, i ^ 1) for i in range(n_wide)]
    n_slots = tenant_node_slot.shape[0]
    span = instruction_node_cache.shape[1]

    own = system_prompt_cache.reshape(-1, 2 * HEAD)
    sib = lax.ppermute(own, "wide", sibling)

    beside = lax.ppermute(queries, "wide", [(i, i ^ 2) for i in range(n_wide)])
    by_head = jnp.transpose(instruction_node_cache, (2, 0, 1, 3))
    beside, by_head = lax.optimization_barrier((beside, by_head))
    nodes = lax.all_to_all(by_head, "narrow", 0, 0, tiled=True)
    nodes = nodes.reshape(n_slots, span, 2 * HEAD)

    pair = jnp.where(
        side == 0,
        jnp.concatenate([queries, beside]),
        jnp.concatenate([beside, queries]),
    )
    pieces = [pair] + [
        lax.ppermute(pair, "wide", [((i + 4 * d) % n_wide, i) for i in range(n_wide)])
        for d in range(1, layers)
    ]
    order = (layer + jnp.arange(layers, dtype=jnp.int32)) % layers

    turned = lax.dynamic_slice_in_dim(
        jnp.concatenate([tenant, tenant]), layer * 4 * rows, n_wide * rows
    ).reshape(chips, 2, rows)
    mine = jnp.where(core == 0, turned[:, 0], turned[:, 1]).reshape(-1)

    kt, ve = _keys(own, sib)
    o_first, lse_first = _system(pieces[:1], kt, ve)
    *pieces[1:], lse_first[0] = lax.optimization_barrier((*pieces[1:], lse_first[0]))
    o_rest, lse_rest = _system(pieces[1:], kt, ve)
    o_sys, lse_sys = [*o_first, *o_rest], [*lse_first, *lse_rest]
    qs, back, table = _plan(tenant_node_slot, mine, pieces)

    o_suf, lse_suf = _suffix(
        suffix_length, queries, suffix_cache.reshape(rows, -1, 2 * HEAD)
    )
    nodes, lse_sys[-1] = lax.optimization_barrier((nodes, lse_sys[-1]))
    nodes_sib = lax.ppermute(nodes, "wide", sibling)
    sent = _node(table, order, qs, back, nodes, nodes_sib, o_sys, lse_sys)
    recv = lax.all_to_all(
        sent.reshape(chips, rows, -1),
        "wide",
        0,
        0,
        axis_index_groups=same_core,
        tiled=True,
    )
    my_tenant = lax.dynamic_slice_in_dim(tenant, position * rows, rows, 0)[:, None]
    parts = _project(
        my_tenant,
        recv,
        o_suf,
        lse_suf,
        output_projection_weight,
        adapter_down_weight,
        n_narrow,
    )
    parts = lax.all_to_all(parts, "narrow", 0, 0, tiled=True)
    return _finish(my_tenant, parts, adapter_up_weight)


def solution(mesh):
    return jax.shard_map(
        per_device,
        mesh=mesh,
        in_specs=(
            P("wide", "narrow"),
            P(),
            P(),
            P("wide"),
            P("wide", "narrow", None),
            P("narrow", "wide", None, None),
            P("wide", None, "narrow", None),
            P("narrow", None),
            P("narrow", None),
            P(None, "narrow"),
        ),
        out_specs=P("wide", "narrow"),
        check_vma=False,
    )
```

```python
import functools

import jax
import jax.numpy as jnp
from jax import lax
from jax.experimental import pallas as pl
from jax.experimental.pallas import tpu as pltpu
from jax.sharding import PartitionSpec as P

HEAD = 128
GROUP = 8
RANK = 16
F32 = jnp.float32
BF16 = jnp.bfloat16
SCALE2 = HEAD**-0.5 * 1.4426950408889634
FLOOR = -1e30
KEY_BLOCK = 2048
HEADS_AT_ONCE = 2
VISIT_ROWS = 16
VISIT_UNROLL = 16


def _params(mib, grid=True):
    return pltpu.CompilerParams(
        vmem_limit_bytes=mib << 20,
        dimension_semantics=("arbitrary",) if grid else None,
    )


def _in_hbm(x):
    return pltpu.with_memory_space_constraint(x, pltpu.HBM)


def _in_vmem(x):
    return pltpu.with_memory_space_constraint(x, pltpu.VMEM)


def _lane(shape):
    return lax.broadcasted_iota(jnp.int32, shape, len(shape) - 1)


def _dot(a, b):
    return jnp.dot(a, b, preferred_element_type=F32)


def _keys_kernel(own_ref, sib_ref, kt_ref, ve_ref):
    n = own_ref.shape[0]
    for i, ref in enumerate((own_ref, sib_ref)):
        at = slice(i * n, (i + 1) * n)
        kt_ref[:, at] = ref[:, :HEAD].T
        ve_ref[at, :HEAD] = ref[:, HEAD:]
        ve_ref[at, HEAD:] = jnp.ones((n, HEAD), BF16)


def _keys(own, sib):
    n = 2 * own.shape[0]
    vmem = pl.BlockSpec(memory_space=pltpu.VMEM)
    return pl.pallas_call(
        _keys_kernel,
        in_specs=[vmem] * 2,
        out_specs=[vmem] * 2,
        out_shape=[
            pltpu.VMEM((HEAD, n), BF16),
            pltpu.VMEM((n, 2 * HEAD), BF16),
        ],
        compiler_params=_params(16, False),
        cost_estimate=pl.CostEstimate(
            flops=0, bytes_accessed=10 * n * HEAD, transcendentals=0
        ),
        name="keys",
    )(own, sib)


def _system_kernel(count, *refs):
    q_hbm, (kt, ve) = refs[:count], refs[count : count + 2]
    o_hbm, lse_hbm = refs[count + 2 : 2 * count + 2], refs[2 * count + 2 : 3 * count + 2]
    q_buf, o_buf, lse_buf, sems = refs[3 * count + 2 :]
    steps = GROUP // HEADS_AT_ONCE
    rows, keys = q_buf.shape[1], kt.shape[1]
    first = [
        pltpu.make_async_copy(q_hbm[b], q_buf.at[b], sems.at[b, steps])
        for b in range(count)
    ]
    for copy in first:
        copy.start()
    lane = _lane((rows, HEAD))
    items = [
        (h, b, k)
        for h in range(HEADS_AT_ONCE)
        for b in range(count)
        for k in range(0, keys, KEY_BLOCK)
    ]
    for b in range(count):
        lse_buf[b] = jnp.zeros((rows, HEAD), F32)
    for copy in first:
        copy.wait()

    def send(b, step):
        width = HEADS_AT_ONCE * HEAD
        at = pl.ds(pl.multiple_of(step * width, width), width)
        return pltpu.make_async_copy(
            o_buf.at[b, :, at], o_hbm[b].at[:, at], sems.at[b, step]
        )

    def some_heads(step, carry):
        def columns(h):
            at = pl.multiple_of((step * HEADS_AT_ONCE + h) * HEAD, HEAD)
            return pl.ds(at, HEAD)

        def score(item):
            h, b, k = item
            return _dot(q_buf[b, :, columns(h)], kt[:, k : k + KEY_BLOCK])

        top, total = {}, {}
        ahead = score(items[0])
        for i, (h, b, k) in enumerate(items):
            s = ahead
            if i + 1 < len(items):
                ahead = score(items[i + 1])
            high = jnp.max(s, axis=1, keepdims=True) * SCALE2
            if (h, b) in top:
                high = jnp.maximum(high, top[h, b])
            p = jnp.exp2(s * SCALE2 - high).astype(BF16)
            r = _dot(p, ve[k : k + KEY_BLOCK, :])
            if (h, b) in top:
                r = total[h, b] * jnp.exp2(top[h, b] - high) + r
            top[h, b], total[h, b] = high, r
        for b in range(count):
            packed = lse_buf[b]
            for h in range(HEADS_AT_ONCE):
                l = total[h, b][:, HEAD:]
                o_buf[b, :, columns(h)] = total[h, b][:, :HEAD] / l
                lse = top[h, b] + jnp.log2(l)
                packed = jnp.where(lane == step * HEADS_AT_ONCE + h, lse, packed)
            lse_buf[b] = packed
            send(b, step).start()
        return carry

    lax.fori_loop(0, steps, some_heads, 0)
    last = [
        pltpu.make_async_copy(lse_buf.at[b], lse_hbm[b], sems.at[b, steps])
        for b in range(count)
    ]
    for copy in last:
        copy.start()
    for b in range(count):
        for step in range(steps):
            send(b, step).wait()
        last[b].wait()


def _system(qs, kt, ve):
    count, rows, keys = len(qs), qs[0].shape[0], ve.shape[0]
    vmem = pl.BlockSpec(memory_space=pltpu.VMEM)
    hbm = pl.BlockSpec(memory_space=pltpu.HBM)
    outs = pl.pallas_call(
        functools.partial(_system_kernel, count),
        in_specs=[hbm] * count + [vmem] * 2,
        out_specs=[hbm] * (2 * count),
        out_shape=[pltpu.HBM((rows, GROUP * HEAD), F32)] * count
        + [pltpu.HBM((rows, HEAD), F32)] * count,
        scratch_shapes=[
            pltpu.VMEM((count, rows, GROUP * HEAD), BF16),
            pltpu.VMEM((count, rows, GROUP * HEAD), F32),
            pltpu.VMEM((count, rows, HEAD), F32),
            pltpu.SemaphoreType.DMA((count, GROUP // HEADS_AT_ONCE + 1)),
        ],
        compiler_params=_params(24, False),
        cost_estimate=pl.CostEstimate(
            flops=6 * count * rows * GROUP * keys * HEAD,
            bytes_accessed=count * rows * 6 * GROUP * HEAD + 6 * keys * HEAD,
            transcendentals=count * rows * GROUP * keys,
        ),
        name="system_attention",
    )(*map(_in_hbm, qs), *map(_in_vmem, [kt, ve]))
    return list(outs[:count]), list(outs[count:])


def _split3(x):
    hi = x.astype(BF16)
    rest = x - hi.astype(F32)
    mid = rest.astype(BF16)
    lo = (rest - mid.astype(F32)).astype(BF16)
    return hi.astype(F32), mid.astype(F32), lo.astype(F32)


def _pack3(x):
    lane = _lane(x.shape)
    hi, mid, lo = _split3(x)
    packed = jnp.where(lane < GROUP, hi, pltpu.roll(mid, GROUP, 1))
    packed = jnp.where(lane < 2 * GROUP, packed, pltpu.roll(lo, 2 * GROUP, 1))
    return jnp.where(lane < 3 * GROUP, packed, 0.0).astype(BF16)


def _unpack3(x):
    return x + (pltpu.roll(x, HEAD - GROUP, 1) + pltpu.roll(x, HEAD - 2 * GROUP, 1))


def _plan_kernel(place, slot_ref, tenant_ref, *refs):
    q_hbm, (qs_ref, back_ref, table_ref, q_buf, sems) = refs[:-5], refs[-5:]
    fetches = [
        pltpu.make_async_copy(ref, q_buf.at[i], sems.at[i])
        for i, ref in enumerate(q_hbm)
    ]
    for fetch in fetches:
        fetch.start()
    rows = qs_ref.shape[0]
    piece = q_buf.shape[1]
    tenants = slot_ref.shape[1]
    width = table_ref.shape[1]

    def iota(shape, dim):
        return lax.broadcasted_iota(jnp.int32, shape, dim)

    def count(where, axis):
        return jnp.sum(where.astype(jnp.int32), axis=axis, keepdims=True)

    chips, both = tenant_ref.shape
    layer, core = place[0], place[1]
    turned = pltpu.roll(tenant_ref[...], (chips - 2 * layer) % chips, 0)
    turned = pltpu.roll(turned, core * (both // 2), 1)
    spread = jnp.concatenate(
        [
            jnp.broadcast_to(turned[j : j + 1, :], (both // 2, both))
            for j in range(chips)
        ],
        axis=0,
    )
    own_lane = iota(spread.shape, 1) == iota(spread.shape, 0) % (both // 2)
    t_col = jnp.sum(jnp.where(own_lane, spread, 0), axis=1, keepdims=True)
    square = iota((rows, rows), 0) == iota((rows, rows), 1)
    t_row = jnp.sum(jnp.where(square, t_col, 0), axis=0, keepdims=True)
    square = iota((tenants, tenants), 0) == iota((tenants, tenants), 1)
    slot_col = jnp.sum(jnp.where(square, slot_ref[...], 0), axis=1, keepdims=True)

    key_row = t_row * rows + iota((1, rows), 1)
    key_col = t_col * rows + iota((rows, 1), 0)
    rank_row = count(key_col < key_row, 0)
    rank_col = count(key_row < key_col, 1)
    to_sorted = (iota((rows, rows), 0) == rank_row).astype(F32).astype(BF16)
    back_ref[...] = (iota((rows, rows), 1) == rank_col).astype(F32).astype(BF16)
    for fetch in fetches:
        fetch.wait()
    qs_ref[...] = sum(
        _dot(to_sorted[:, i * piece : (i + 1) * piece], q_buf[i])
        for i in range(len(fetches))
    ).astype(BF16)

    def visits_of(low, high):
        first = low // VISIT_ROWS
        last = (high + VISIT_ROWS - 1) // VISIT_ROWS
        return first, jnp.where(high > low, last - first, 0)

    lane = iota((1, width), 1)
    _, n_row = visits_of(count(t_col < lane, 0), count(t_col < lane + 1, 0))
    t = iota((tenants, 1), 0)
    low, high = count(t_row < t, 1), count(t_row < t + 1, 1)
    first, n = visits_of(low, high)
    start = jnp.sum(jnp.where(lane < t, n_row, 0), axis=1, keepdims=True)
    here = (lane >= start) & (lane < start + n)

    def pick(column):
        return jnp.sum(jnp.where(here, column, 0), axis=0, keepdims=True)

    table_ref[...] = jnp.concatenate(
        [
            pick(first - start + lane),
            pick(slot_col),
            pick(low),
            pick(high),
            jnp.broadcast_to(jnp.sum(n, axis=0, keepdims=True), (1, width)),
        ]
        + [jnp.zeros((1, width), jnp.int32)] * 3,
        axis=0,
    )


def _plan(place, slots, tenant, qs):
    rows, width = sum(q.shape[0] for q in qs), qs[0].shape[1]
    chips = 2 * len(qs)
    vmem = pl.BlockSpec(memory_space=pltpu.VMEM)
    return pl.pallas_call(
        _plan_kernel,
        in_specs=[pl.BlockSpec(memory_space=pltpu.SMEM)]
        + [vmem] * 2
        + [pl.BlockSpec(memory_space=pltpu.HBM)] * len(qs),
        out_specs=[vmem] * 3,
        out_shape=[
            pltpu.VMEM((rows, width), BF16),
            pltpu.VMEM((rows, rows), BF16),
            jax.ShapeDtypeStruct((8, HEAD), jnp.int32),
        ],
        scratch_shapes=[
            pltpu.VMEM((len(qs), *qs[0].shape), BF16),
            pltpu.SemaphoreType.DMA((len(qs),)),
        ],
        compiler_params=_params(16, False),
        cost_estimate=pl.CostEstimate(
            flops=2 * rows * rows * width,
            bytes_accessed=6 * rows * width,
            transcendentals=0,
        ),
        name="plan",
    )(place, slots[None, :], tenant.reshape(chips, -1), *map(_in_hbm, qs))


def _node_kernel(count, table, place, qs, back_ref, own_ref, sib_ref, *refs):
    o_hbm, lse_hbm = refs[:count], refs[count : 2 * count]
    out_ref, on, lse_n, o_buf, lse_buf, done, sems = refs[2 * count :]
    fetches = []
    for i in range(count):
        fetches += [
            pltpu.make_async_copy(o_hbm[i], o_buf.at[i], sems.at[i]),
            pltpu.make_async_copy(lse_hbm[i], lse_buf.at[i], sems.at[count + i]),
        ]
    for fetch in fetches:
        fetch.start()
    vr = VISIT_ROWS
    lane = _lane((vr, HEAD))
    row_in_block = lax.broadcasted_iota(jnp.int32, (vr, HEAD), 0)
    dims = (((1,), (1,)), ((), ()))

    def step(i, carry):
        blocks, spans, scores, slots = [], [], [], []
        for u in range(VISIT_UNROLL):
            v = i * VISIT_UNROLL + u
            at = pl.ds(pl.multiple_of(table[0, v] * vr, vr), vr)
            slot = table[1, v]
            qb = jnp.concatenate(
                [qs[at, g * HEAD : (g + 1) * HEAD] for g in range(GROUP)], axis=0
            )
            scores.append(
                [
                    lax.dot_general(
                        qb, ref[slot, :, :HEAD], dims, preferred_element_type=F32
                    )
                    for ref in (own_ref, sib_ref)
                ]
            )
            blocks.append(at)
            slots.append(slot)
            row = row_in_block + table[0, v] * vr
            spans.append((row >= table[2, v]) & (row < table[3, v]))
        tops, parts = [], []
        for s0, s1 in scores:
            high = jnp.max(jnp.maximum(s0, s1), axis=1, keepdims=True) * SCALE2
            p0 = jnp.exp2(s0 * SCALE2 - high)
            p1 = jnp.exp2(s1 * SCALE2 - high)
            tops.append(high)
            parts.append((p0, p1))
        results = []
        for (p0, p1), slot in zip(parts, slots):
            l = jnp.sum(p0 + p1, axis=1, keepdims=True)
            r = _dot(p0.astype(BF16), own_ref[slot, :, HEAD:]) + _dot(
                p1.astype(BF16), sib_ref[slot, :, HEAD:]
            )
            results.append((r, l))
        for at, inside, high, (r, l) in zip(blocks, spans, tops, results):
            o = r / l
            lse = high + jnp.log2(l)
            packed = jnp.zeros((vr, HEAD), F32)
            for g in range(GROUP):
                sub = slice(g * vr, (g + 1) * vr)
                cols = slice(g * HEAD, (g + 1) * HEAD)
                on[at, cols] = jnp.where(inside, o[sub, :], on[at, cols].astype(F32)).astype(
                    BF16
                )
                packed = jnp.where(lane == g, lse[sub, :], packed)
            lse_n[at, :] = jnp.where(inside, packed, lse_n[at, :])
        return carry

    lax.fori_loop(0, (table[4, 0] + VISIT_UNROLL - 1) // VISIT_UNROLL, step, 0)

    packed_lse = _pack3(lse_n[...])
    piece = done.shape[1]
    sends = []
    for i in range(count):
        back = back_ref[i * piece : (i + 1) * piece, :]
        lse_node = _unpack3(_dot(back, packed_lse))
        o_node = _dot(back, on[...])
        fetches[2 * i].wait()
        fetches[2 * i + 1].wait()
        lse_sys = lse_buf[i]
        top = jnp.maximum(lse_sys, lse_node)
        w_sys, w_node = jnp.exp2(lse_sys - top), jnp.exp2(lse_node - top)
        z = w_sys + w_node
        done[i, :, GROUP * HEAD :] = _pack3(top + jnp.log2(z))
        w_node = w_node / z
        for g in range(GROUP):
            cols = slice(g * HEAD, (g + 1) * HEAD)
            o_sys = o_buf[i, :, cols]
            o = o_sys + w_node[:, g : g + 1] * (o_node[:, cols] - o_sys)
            done[i, :, cols] = o.astype(BF16)
        layer = lax.rem(place[0] + i, count)
        to = pl.ds(pl.multiple_of(layer * piece, piece), piece)
        send = pltpu.make_async_copy(done.at[i], out_ref.at[to], sems.at[2 * count + i])
        send.start()
        sends.append(send)
    for send in sends:
        send.wait()


def _node(table, place, qs, back, own, sib, o_sys, lse_sys):
    rows, count = qs.shape[0], len(o_sys)
    smem = pl.BlockSpec(memory_space=pltpu.SMEM)
    hbm = pl.BlockSpec(memory_space=pltpu.HBM)
    piece = o_sys[0].shape[0]
    vmem = pl.BlockSpec(memory_space=pltpu.VMEM)
    return pl.pallas_call(
        functools.partial(_node_kernel, count),
        in_specs=[smem] * 2 + [vmem] * 4 + [hbm] * (2 * count),
        out_specs=hbm,
        out_shape=pltpu.HBM((rows, (GROUP + 1) * HEAD), BF16),
        scratch_shapes=[
            pltpu.VMEM((rows, GROUP * HEAD), BF16),
            pltpu.VMEM((rows, HEAD), F32),
            pltpu.VMEM((count, piece, GROUP * HEAD), F32),
            pltpu.VMEM((count, piece, HEAD), F32),
            pltpu.VMEM((count, piece, (GROUP + 1) * HEAD), BF16),
            pltpu.SemaphoreType.DMA((3 * count,)),
        ],
        compiler_params=_params(24, False),
        cost_estimate=pl.CostEstimate(
            flops=2 * 10**9, bytes_accessed=8 * 2**20, transcendentals=2**20
        ),
        name="node_attention",
    )(
        table,
        place,
        *map(_in_vmem, [qs, back, own, sib]),
        *map(_in_hbm, [*o_sys, *lse_sys]),
    )


def _suffix_kernel(len_ref, q_ref, kv_hbm, o_ref, lse_ref, kv_ref, sems):
    rows, span = kv_ref.shape[0], kv_ref.shape[1]
    block = rows // sems.shape[0]
    fetches = [
        pltpu.make_async_copy(
            kv_hbm.at[pl.ds(i * block, block)],
            kv_ref.at[pl.ds(i * block, block)],
            sems.at[i],
        )
        for i in range(sems.shape[0])
    ]
    for fetch in fetches:
        fetch.start()
    position = _lane((GROUP, span))
    dims = (((1,), (1,)), ((), ()))
    for i, fetch in enumerate(fetches):
        fetch.wait()
        here = range(i * block, (i + 1) * block)
        scores = [
            lax.dot_general(
                q_ref[r], kv_ref[r, :, :HEAD], dims, preferred_element_type=F32
            )
            for r in here
        ]
        parts = []
        for r, s in zip(here, scores):
            usable = position < len_ref[r]
            s = jnp.where(usable, s * SCALE2, FLOOR)
            high = jnp.max(s, axis=1, keepdims=True)
            p = jnp.where(usable, jnp.exp2(s - high), 0.0)
            parts.append((p, high, jnp.sum(p, axis=1, keepdims=True)))
        for r, (p, high, l) in zip(here, parts):
            o_ref[r] = _dot(p.astype(BF16), kv_ref[r, :, HEAD:]) / l
            lse_ref[r] = jnp.broadcast_to(high + jnp.log2(l), (GROUP, HEAD))


def _suffix(lengths, q, kv):
    rows, span = kv.shape[0], kv.shape[1]
    shape = jax.ShapeDtypeStruct((rows, GROUP, HEAD), F32)
    vmem = pl.BlockSpec(memory_space=pltpu.VMEM)
    return pl.pallas_call(
        _suffix_kernel,
        in_specs=[
            pl.BlockSpec(memory_space=pltpu.SMEM),
            vmem,
            pl.BlockSpec(memory_space=pltpu.HBM),
        ],
        out_specs=[vmem, vmem],
        out_shape=[shape, shape],
        scratch_shapes=[
            pltpu.VMEM(kv.shape, BF16),
            pltpu.SemaphoreType.DMA((8,)),
        ],
        compiler_params=_params(24, False),
        cost_estimate=pl.CostEstimate(
            flops=10**9, bytes_accessed=rows * span * 512, transcendentals=2**17
        ),
        name="suffix_attention",
    )(lengths, q.reshape(rows, GROUP, HEAD), _in_hbm(kv))


def _project_kernel(
    tenant_ref,
    recv_ref,
    o_ref,
    lse_ref,
    w_hbm,
    down_hbm,
    out_ref,
    att,
    low,
    w_ref,
    down_ref,
    sems,
):
    parts, rows = recv_ref.shape[0], recv_ref.shape[1]
    step = pl.program_id(0)
    width = w_ref.shape[2]

    def fetch_w(d):
        at = pl.multiple_of(d * width, HEAD)
        return pltpu.make_async_copy(
            w_hbm.at[:, pl.ds(at, width)], w_ref.at[d], sems.at[d]
        )

    fetch_down = pltpu.make_async_copy(down_hbm, down_ref, sems.at[w_ref.shape[0]])

    @pl.when(step == 0)
    def _():
        fetch_down.start()
        for d in range(w_ref.shape[0]):
            fetch_w(d).start()
        lane = _lane((rows, HEAD))
        own = jnp.zeros((rows, HEAD), F32)
        for g in range(GROUP):
            own = jnp.where(lane == g, lse_ref[:, g, :], own)
        lses = [own] + [
            _unpack3(recv_ref[w, :, GROUP * HEAD :].astype(F32)) for w in range(parts)
        ]
        top = functools.reduce(jnp.maximum, lses)
        weights = [jnp.exp2(x - top) for x in lses]
        z = functools.reduce(jnp.add, weights)
        weights = [x / z for x in weights]
        for g in range(GROUP):
            cols = slice(g * HEAD, (g + 1) * HEAD)
            acc = weights[0][:, g : g + 1] * o_ref[:, g, :]
            for w in range(parts):
                acc += weights[1 + w][:, g : g + 1] * recv_ref[w, :, cols].astype(F32)
            att[:, cols] = acc.astype(BF16)
        fetch_down.wait()
        reduced = _dot(att[...], down_ref[...])
        mine = _lane(reduced.shape) // RANK == tenant_ref[...]
        reduced = jnp.where(mine, reduced, 0.0)
        kept = reduced[:, :HEAD]
        for c in range(HEAD, reduced.shape[1], HEAD):
            kept = kept + reduced[:, c : c + HEAD]
        low[...] = kept.astype(BF16)

    fetch_w(step).wait()
    out_ref[0, :, :width] = _dot(att[...], w_ref[step]).astype(BF16)
    out_ref[0, :, width:] = low[...]


def _project(tenant, recv, o, lse, weight, down, parts):
    rows = recv.shape[1]
    depth, features = weight.shape
    width = features // parts

    def whole(shape):
        return pl.BlockSpec(shape, lambda d: (0,) * len(shape))

    return pl.pallas_call(
        _project_kernel,
        grid=(parts,),
        in_specs=[
            whole((rows, 1)),
            whole(recv.shape),
            whole(o.shape),
            whole(lse.shape),
            pl.BlockSpec(memory_space=pltpu.HBM),
            pl.BlockSpec(memory_space=pltpu.HBM),
        ],
        out_specs=pl.BlockSpec((1, rows, width + HEAD), lambda d: (d, 0, 0)),
        out_shape=jax.ShapeDtypeStruct((parts, rows, width + HEAD), BF16),
        scratch_shapes=[
            pltpu.VMEM((rows, GROUP * HEAD), BF16),
            pltpu.VMEM((rows, HEAD), BF16),
            pltpu.VMEM((parts, depth, width), BF16),
            pltpu.VMEM(down.shape, BF16),
            pltpu.SemaphoreType.DMA((parts + 1,)),
        ],
        compiler_params=_params(32),
        cost_estimate=pl.CostEstimate(
            flops=2 * rows * depth * features,
            bytes_accessed=2 * depth * features,
            transcendentals=0,
        ),
        name="project",
    )(tenant, recv, o, lse, _in_hbm(weight), _in_hbm(down))


def _finish_kernel(tenant_ref, recv_ref, up_ref, out_ref):
    parts, rows = recv_ref.shape[0], recv_ref.shape[1]
    width = out_ref.shape[1]
    total = recv_ref[0].astype(F32)
    for w in range(1, parts):
        total += recv_ref[w].astype(F32)
    depth = up_ref.shape[0]
    low = jnp.concatenate([total[:, width:]] * (depth // HEAD), axis=1)
    mine = _lane((rows, depth)) // RANK == tenant_ref[...]
    chosen = jnp.where(mine, low, 0.0).astype(BF16)
    out_ref[...] = (total[:, :width] + _dot(chosen, up_ref[...])).astype(BF16)


def _finish(tenant, recv, up):
    vmem = pl.BlockSpec(memory_space=pltpu.VMEM)
    return pl.pallas_call(
        _finish_kernel,
        in_specs=[vmem] * 3,
        out_specs=vmem,
        out_shape=jax.ShapeDtypeStruct((recv.shape[1], up.shape[1]), BF16),
        compiler_params=_params(16, False),
        name="finish",
    )(tenant, recv, up)


def per_device(
    queries,
    tenant,
    tenant_node_slot,
    suffix_length,
    system_prompt_cache,
    instruction_node_cache,
    suffix_cache,
    output_projection_weight,
    adapter_down_weight,
    adapter_up_weight,
):
    rows, width = queries.shape
    n_wide = lax.axis_size("wide")
    n_narrow = lax.axis_size("narrow")
    chips = n_wide // 2
    layers = chips // 2
    position = lax.axis_index("wide")
    layer, side, core = position // 4, position // 2 % 2, position % 2
    same_core = [[2 * j + c for j in range(chips)] for c in range(2)]
    sibling = [(i, i ^ 1) for i in range(n_wide)]
    n_slots = tenant_node_slot.shape[0]
    span = instruction_node_cache.shape[1]

    own = system_prompt_cache.reshape(-1, 2 * HEAD)
    sib = lax.ppermute(own, "wide", sibling)

    beside = lax.ppermute(queries, "wide", [(i, i ^ 2) for i in range(n_wide)])
    by_head = jnp.transpose(instruction_node_cache, (2, 0, 1, 3))
    place = jnp.stack([layer, core])
    beside, by_head, place = lax.optimization_barrier((beside, by_head, place))
    nodes = lax.all_to_all(by_head, "narrow", 0, 0, tiled=True)
    nodes = nodes.reshape(n_slots, span, 2 * HEAD)

    pair = jnp.where(
        side == 0,
        jnp.concatenate([queries, beside]),
        jnp.concatenate([beside, queries]),
    )
    pieces = [pair] + [
        lax.ppermute(pair, "wide", [((i + 4 * d) % n_wide, i) for i in range(n_wide)])
        for d in range(1, layers)
    ]
    kt, ve = _keys(own, sib)
    o_a, lse_a = _system(pieces[:1], kt, ve)
    *pieces[1:], lse_a[0] = lax.optimization_barrier((*pieces[1:], lse_a[0]))
    o_b, lse_b = _system(pieces[1:], kt, ve)
    o_sys, lse_sys = [*o_a, *o_b], [*lse_a, *lse_b]
    nodes, lse_sys[-1], *pieces = lax.optimization_barrier(
        (nodes, lse_sys[-1], *pieces)
    )
    nodes_sib = lax.ppermute(nodes, "wide", sibling)
    qs, back, table = _plan(place, tenant_node_slot, tenant, pieces)

    o_suf, lse_suf = _suffix(
        suffix_length, queries, suffix_cache.reshape(rows, -1, 2 * HEAD)
    )
    sent = _node(table, place, qs, back, nodes, nodes_sib, o_sys, lse_sys)
    recv = lax.all_to_all(
        sent.reshape(chips, rows, -1),
        "wide",
        0,
        0,
        axis_index_groups=same_core,
        tiled=True,
    )
    my_tenant = lax.dynamic_slice_in_dim(tenant, position * rows, rows, 0)[:, None]
    parts = _project(
        my_tenant,
        recv,
        o_suf,
        lse_suf,
        output_projection_weight,
        adapter_down_weight,
        n_narrow,
    )
    parts = lax.all_to_all(parts, "narrow", 0, 0, tiled=True)
    return _finish(my_tenant, parts, adapter_up_weight)


def solution(mesh):
    return jax.shard_map(
        per_device,
        mesh=mesh,
        in_specs=(
            P("wide", "narrow"),
            P(),
            P(),
            P("wide"),
            P("wide", "narrow", None),
            P("narrow", "wide", None, None),
            P("wide", None, "narrow", None),
            P("narrow", None),
            P("narrow", None),
            P(None, "narrow"),
        ),
        out_specs=P("wide", "narrow"),
        check_vma=False,
    )
```

```python
import functools

import jax
import jax.numpy as jnp
from jax import lax
from jax.experimental import pallas as pl
from jax.experimental.pallas import tpu as pltpu
from jax.sharding import PartitionSpec as P

HEAD = 128
GROUP = 8
RANK = 16
F32 = jnp.float32
BF16 = jnp.bfloat16
SCALE2 = HEAD**-0.5 * 1.4426950408889634
FLOOR = -1e30
KEY_BLOCK = 512
ONES = 16
VISIT_ROWS = 16
VISIT_UNROLL = 16


def _params(mib, grid=True):
    return pltpu.CompilerParams(
        vmem_limit_bytes=mib << 20,
        dimension_semantics=("arbitrary",) if grid else None,
    )


def _in_hbm(x):
    return pltpu.with_memory_space_constraint(x, pltpu.HBM)


def _in_vmem(x):
    return pltpu.with_memory_space_constraint(x, pltpu.VMEM)


def _lane(shape):
    return lax.broadcasted_iota(jnp.int32, shape, len(shape) - 1)


def _dot(a, b):
    return jnp.dot(a, b, preferred_element_type=F32)


def _keys_kernel(own_ref, sib_ref, k_ref, vt_ref):
    n = own_ref.shape[0]
    for i, ref in enumerate((own_ref, sib_ref)):
        at = slice(i * n, (i + 1) * n)
        k_ref[at, :] = ref[:, :HEAD]
        vt_ref[:HEAD, at] = ref[:, HEAD:].T
    vt_ref[HEAD:, :] = jnp.ones((ONES, 2 * n), BF16)


def _keys(own, sib):
    n = 2 * own.shape[0]
    vmem = pl.BlockSpec(memory_space=pltpu.VMEM)
    return pl.pallas_call(
        _keys_kernel,
        in_specs=[vmem] * 2,
        out_specs=[vmem] * 2,
        out_shape=[
            pltpu.VMEM((n, HEAD), BF16),
            pltpu.VMEM((HEAD + ONES, n), BF16),
        ],
        compiler_params=_params(16, False),
        cost_estimate=pl.CostEstimate(
            flops=0, bytes_accessed=8 * n * HEAD, transcendentals=0
        ),
        name="keys",
    )(own, sib)


def _system_kernel(count, *refs):
    q_hbm, (k_ref, vt_ref) = refs[:count], refs[count : count + 2]
    o_hbm, lse_hbm = refs[count + 2 : 2 * count + 2], refs[2 * count + 2 : 3 * count + 2]
    q_buf, qt, o_buf, lse_buf, sems = refs[3 * count + 2 :]
    rows, keys = q_buf.shape[1], k_ref.shape[0]
    heads = [slice(g * HEAD, (g + 1) * HEAD) for g in range(GROUP)]
    across = [slice(g * rows, (g + 1) * rows) for g in range(GROUP)]
    first = [
        pltpu.make_async_copy(q_hbm[b], q_buf.at[b], sems.at[b, 0])
        for b in range(count)
    ]
    for copy in first:
        copy.start()
    for b in range(count):
        first[b].wait()
        for g in range(GROUP):
            qt[b, :, across[g]] = q_buf[b, :, heads[g]].T
    items = [(b, k) for b in range(count) for k in range(0, keys, KEY_BLOCK)]

    def score(item):
        b, k = item
        return _dot(k_ref[k : k + KEY_BLOCK, :], qt[b])

    last = []
    top = total = None
    ahead = score(items[0])
    for i, (b, k) in enumerate(items):
        s = ahead
        if i + 1 < len(items):
            ahead = score(items[i + 1])
        high = jnp.max(s, axis=0, keepdims=True) * SCALE2
        if k:
            high = jnp.maximum(high, top)
        p = jnp.exp2(s * SCALE2 - high).astype(BF16)
        r = _dot(vt_ref[:, k : k + KEY_BLOCK], p)
        total = total * jnp.exp2(top - high) + r if k else r
        top = high
        if k + KEY_BLOCK < keys:
            continue
        l = total[HEAD : HEAD + 1, :]
        o = total[:HEAD, :] / l
        lse = top + jnp.log2(l)
        for g in range(GROUP):
            o_buf[b, :, heads[g]] = o[:, across[g]].T
        lse = jnp.concatenate(
            [lse[:, across[g]] for g in range(GROUP)]
            + [jnp.zeros((HEAD - GROUP, rows), F32)],
            axis=0,
        )
        lse_buf[b] = lse.T
        for j, (src, dst) in enumerate([(o_buf, o_hbm), (lse_buf, lse_hbm)]):
            copy = pltpu.make_async_copy(src.at[b], dst[b], sems.at[b, 1 + j])
            copy.start()
            last.append(copy)
    for copy in last:
        copy.wait()


def _system(qs, k, vt):
    count, rows, keys = len(qs), qs[0].shape[0], k.shape[0]
    vmem = pl.BlockSpec(memory_space=pltpu.VMEM)
    hbm = pl.BlockSpec(memory_space=pltpu.HBM)
    outs = pl.pallas_call(
        functools.partial(_system_kernel, count),
        in_specs=[hbm] * count + [vmem] * 2,
        out_specs=[hbm] * (2 * count),
        out_shape=[pltpu.HBM((rows, GROUP * HEAD), F32)] * count
        + [pltpu.HBM((rows, HEAD), F32)] * count,
        scratch_shapes=[
            pltpu.VMEM((count, rows, GROUP * HEAD), BF16),
            pltpu.VMEM((count, HEAD, GROUP * rows), BF16),
            pltpu.VMEM((count, rows, GROUP * HEAD), F32),
            pltpu.VMEM((count, rows, HEAD), F32),
            pltpu.SemaphoreType.DMA((count, 3)),
        ],
        compiler_params=_params(40, False),
        cost_estimate=pl.CostEstimate(
            flops=6 * count * rows * GROUP * keys * HEAD,
            bytes_accessed=count * rows * 6 * GROUP * HEAD + 6 * keys * HEAD,
            transcendentals=count * rows * GROUP * keys,
        ),
        name="system_attention",
    )(*map(_in_hbm, qs), *map(_in_vmem, [k, vt]))
    return list(outs[:count]), list(outs[count:])


def _split3(x):
    hi = x.astype(BF16)
    rest = x - hi.astype(F32)
    mid = rest.astype(BF16)
    lo = (rest - mid.astype(F32)).astype(BF16)
    return hi.astype(F32), mid.astype(F32), lo.astype(F32)


def _pack3(x):
    lane = _lane(x.shape)
    hi, mid, lo = _split3(x)
    packed = jnp.where(lane < GROUP, hi, pltpu.roll(mid, GROUP, 1))
    packed = jnp.where(lane < 2 * GROUP, packed, pltpu.roll(lo, 2 * GROUP, 1))
    return jnp.where(lane < 3 * GROUP, packed, 0.0).astype(BF16)


def _unpack3(x):
    return x + (pltpu.roll(x, HEAD - GROUP, 1) + pltpu.roll(x, HEAD - 2 * GROUP, 1))


def _plan_kernel(place, slot_ref, tenant_ref, *refs):
    q_hbm, (qs_ref, back_ref, table_ref, q_buf, sems) = refs[:-5], refs[-5:]
    fetches = [
        pltpu.make_async_copy(ref, q_buf.at[i], sems.at[i])
        for i, ref in enumerate(q_hbm)
    ]
    for fetch in fetches:
        fetch.start()
    rows = qs_ref.shape[0]
    piece = q_buf.shape[1]
    tenants = slot_ref.shape[1]
    width = table_ref.shape[1]

    def iota(shape, dim):
        return lax.broadcasted_iota(jnp.int32, shape, dim)

    def count(where, axis):
        return jnp.sum(where.astype(jnp.int32), axis=axis, keepdims=True)

    chips, both = tenant_ref.shape
    layer, core = place[0], place[1]
    turned = pltpu.roll(tenant_ref[...], (chips - 2 * layer) % chips, 0)
    turned = pltpu.roll(turned, core * (both // 2), 1)
    spread = jnp.concatenate(
        [
            jnp.broadcast_to(turned[j : j + 1, :], (both // 2, both))
            for j in range(chips)
        ],
        axis=0,
    )
    own_lane = iota(spread.shape, 1) == iota(spread.shape, 0) % (both // 2)
    t_col = jnp.sum(jnp.where(own_lane, spread, 0), axis=1, keepdims=True)
    square = iota((rows, rows), 0) == iota((rows, rows), 1)
    t_row = jnp.sum(jnp.where(square, t_col, 0), axis=0, keepdims=True)
    square = iota((tenants, tenants), 0) == iota((tenants, tenants), 1)
    slot_col = jnp.sum(jnp.where(square, slot_ref[...], 0), axis=1, keepdims=True)

    key_row = t_row * rows + iota((1, rows), 1)
    key_col = t_col * rows + iota((rows, 1), 0)
    rank_row = count(key_col < key_row, 0)
    rank_col = count(key_row < key_col, 1)
    to_sorted = (iota((rows, rows), 0) == rank_row).astype(F32).astype(BF16)
    back_ref[...] = (iota((rows, rows), 1) == rank_col).astype(F32).astype(BF16)
    for fetch in fetches:
        fetch.wait()
    qs_ref[...] = sum(
        _dot(to_sorted[:, i * piece : (i + 1) * piece], q_buf[i])
        for i in range(len(fetches))
    ).astype(BF16)

    def visits_of(low, high):
        first = low // VISIT_ROWS
        last = (high + VISIT_ROWS - 1) // VISIT_ROWS
        return first, jnp.where(high > low, last - first, 0)

    lane = iota((1, width), 1)
    _, n_row = visits_of(count(t_col < lane, 0), count(t_col < lane + 1, 0))
    t = iota((tenants, 1), 0)
    low, high = count(t_row < t, 1), count(t_row < t + 1, 1)
    first, n = visits_of(low, high)
    start = jnp.sum(jnp.where(lane < t, n_row, 0), axis=1, keepdims=True)
    here = (lane >= start) & (lane < start + n)

    def pick(column):
        return jnp.sum(jnp.where(here, column, 0), axis=0, keepdims=True)

    table_ref[...] = jnp.concatenate(
        [
            pick(first - start + lane),
            pick(slot_col),
            pick(low),
            pick(high),
            jnp.broadcast_to(jnp.sum(n, axis=0, keepdims=True), (1, width)),
        ]
        + [jnp.zeros((1, width), jnp.int32)] * 3,
        axis=0,
    )


def _plan(place, slots, tenant, qs):
    rows, width = sum(q.shape[0] for q in qs), qs[0].shape[1]
    chips = 2 * len(qs)
    vmem = pl.BlockSpec(memory_space=pltpu.VMEM)
    return pl.pallas_call(
        _plan_kernel,
        in_specs=[pl.BlockSpec(memory_space=pltpu.SMEM)]
        + [vmem] * 2
        + [pl.BlockSpec(memory_space=pltpu.HBM)] * len(qs),
        out_specs=[vmem] * 3,
        out_shape=[
            pltpu.VMEM((rows, width), BF16),
            pltpu.VMEM((rows, rows), BF16),
            jax.ShapeDtypeStruct((8, HEAD), jnp.int32),
        ],
        scratch_shapes=[
            pltpu.VMEM((len(qs), *qs[0].shape), BF16),
            pltpu.SemaphoreType.DMA((len(qs),)),
        ],
        compiler_params=_params(16, False),
        cost_estimate=pl.CostEstimate(
            flops=2 * rows * rows * width,
            bytes_accessed=6 * rows * width,
            transcendentals=0,
        ),
        name="plan",
    )(place, slots[None, :], tenant.reshape(chips, -1), *map(_in_hbm, qs))


def _node_kernel(count, table, place, qs, back_ref, own_ref, sib_ref, *refs):
    o_hbm, lse_hbm = refs[:count], refs[count : 2 * count]
    out_ref, on, lse_n, o_buf, lse_buf, done, sems = refs[2 * count :]
    fetches = []
    for i in range(count):
        fetches += [
            pltpu.make_async_copy(o_hbm[i], o_buf.at[i], sems.at[i]),
            pltpu.make_async_copy(lse_hbm[i], lse_buf.at[i], sems.at[count + i]),
        ]
    for fetch in fetches:
        fetch.start()
    vr = VISIT_ROWS
    lane = _lane((vr, HEAD))
    row_in_block = lax.broadcasted_iota(jnp.int32, (vr, HEAD), 0)
    dims = (((1,), (1,)), ((), ()))

    def step(i, carry):
        blocks, spans, scores, slots = [], [], [], []
        for u in range(VISIT_UNROLL):
            v = i * VISIT_UNROLL + u
            at = pl.ds(pl.multiple_of(table[0, v] * vr, vr), vr)
            slot = table[1, v]
            qb = jnp.concatenate(
                [qs[at, g * HEAD : (g + 1) * HEAD] for g in range(GROUP)], axis=0
            )
            scores.append(
                [
                    lax.dot_general(
                        qb, ref[slot, :, :HEAD], dims, preferred_element_type=F32
                    )
                    for ref in (own_ref, sib_ref)
                ]
            )
            blocks.append(at)
            slots.append(slot)
            row = row_in_block + table[0, v] * vr
            spans.append((row >= table[2, v]) & (row < table[3, v]))
        tops, parts = [], []
        for s0, s1 in scores:
            high = jnp.max(jnp.maximum(s0, s1), axis=1, keepdims=True) * SCALE2
            p0 = jnp.exp2(s0 * SCALE2 - high)
            p1 = jnp.exp2(s1 * SCALE2 - high)
            tops.append(high)
            parts.append((p0, p1))
        results = []
        for (p0, p1), slot in zip(parts, slots):
            l = jnp.sum(p0 + p1, axis=1, keepdims=True)
            r = _dot(p0.astype(BF16), own_ref[slot, :, HEAD:]) + _dot(
                p1.astype(BF16), sib_ref[slot, :, HEAD:]
            )
            results.append((r, l))
        for at, inside, high, (r, l) in zip(blocks, spans, tops, results):
            o = r / l
            lse = high + jnp.log2(l)
            packed = jnp.zeros((vr, HEAD), F32)
            for g in range(GROUP):
                sub = slice(g * vr, (g + 1) * vr)
                cols = slice(g * HEAD, (g + 1) * HEAD)
                on[at, cols] = jnp.where(inside, o[sub, :], on[at, cols].astype(F32)).astype(
                    BF16
                )
                packed = jnp.where(lane == g, lse[sub, :], packed)
            lse_n[at, :] = jnp.where(inside, packed, lse_n[at, :])
        return carry

    lax.fori_loop(0, (table[4, 0] + VISIT_UNROLL - 1) // VISIT_UNROLL, step, 0)

    packed_lse = _pack3(lse_n[...])
    piece = done.shape[1]
    sends = []
    for i in range(count):
        back = back_ref[i * piece : (i + 1) * piece, :]
        lse_node = _unpack3(_dot(back, packed_lse))
        o_node = _dot(back, on[...])
        fetches[2 * i].wait()
        fetches[2 * i + 1].wait()
        lse_sys = lse_buf[i]
        top = jnp.maximum(lse_sys, lse_node)
        w_sys, w_node = jnp.exp2(lse_sys - top), jnp.exp2(lse_node - top)
        z = w_sys + w_node
        done[i, :, GROUP * HEAD :] = _pack3(top + jnp.log2(z))
        w_node = w_node / z
        for g in range(GROUP):
            cols = slice(g * HEAD, (g + 1) * HEAD)
            o_sys = o_buf[i, :, cols]
            o = o_sys + w_node[:, g : g + 1] * (o_node[:, cols] - o_sys)
            done[i, :, cols] = o.astype(BF16)
        layer = lax.rem(place[0] + i, count)
        to = pl.ds(pl.multiple_of(layer * piece, piece), piece)
        send = pltpu.make_async_copy(done.at[i], out_ref.at[to], sems.at[2 * count + i])
        send.start()
        sends.append(send)
    for send in sends:
        send.wait()


def _node(table, place, qs, back, own, sib, o_sys, lse_sys):
    rows, count = qs.shape[0], len(o_sys)
    smem = pl.BlockSpec(memory_space=pltpu.SMEM)
    hbm = pl.BlockSpec(memory_space=pltpu.HBM)
    piece = o_sys[0].shape[0]
    vmem = pl.BlockSpec(memory_space=pltpu.VMEM)
    return pl.pallas_call(
        functools.partial(_node_kernel, count),
        in_specs=[smem] * 2 + [vmem] * 4 + [hbm] * (2 * count),
        out_specs=hbm,
        out_shape=pltpu.HBM((rows, (GROUP + 1) * HEAD), BF16),
        scratch_shapes=[
            pltpu.VMEM((rows, GROUP * HEAD), BF16),
            pltpu.VMEM((rows, HEAD), F32),
            pltpu.VMEM((count, piece, GROUP * HEAD), F32),
            pltpu.VMEM((count, piece, HEAD), F32),
            pltpu.VMEM((count, piece, (GROUP + 1) * HEAD), BF16),
            pltpu.SemaphoreType.DMA((3 * count,)),
        ],
        compiler_params=_params(24, False),
        cost_estimate=pl.CostEstimate(
            flops=2 * 10**9, bytes_accessed=8 * 2**20, transcendentals=2**20
        ),
        name="node_attention",
    )(
        table,
        place,
        *map(_in_vmem, [qs, back, own, sib]),
        *map(_in_hbm, [*o_sys, *lse_sys]),
    )


def _suffix_kernel(len_ref, q_ref, kv_hbm, o_ref, lse_ref, kv_ref, sems):
    rows, span = kv_ref.shape[0], kv_ref.shape[1]
    block = rows // sems.shape[0]
    fetches = [
        pltpu.make_async_copy(
            kv_hbm.at[pl.ds(i * block, block)],
            kv_ref.at[pl.ds(i * block, block)],
            sems.at[i],
        )
        for i in range(sems.shape[0])
    ]
    for fetch in fetches:
        fetch.start()
    position = _lane((GROUP, span))
    dims = (((1,), (1,)), ((), ()))
    for i, fetch in enumerate(fetches):
        fetch.wait()
        here = range(i * block, (i + 1) * block)
        scores = [
            lax.dot_general(
                q_ref[r], kv_ref[r, :, :HEAD], dims, preferred_element_type=F32
            )
            for r in here
        ]
        parts = []
        for r, s in zip(here, scores):
            usable = position < len_ref[r]
            s = jnp.where(usable, s * SCALE2, FLOOR)
            high = jnp.max(s, axis=1, keepdims=True)
            p = jnp.where(usable, jnp.exp2(s - high), 0.0)
            parts.append((p, high, jnp.sum(p, axis=1, keepdims=True)))
        for r, (p, high, l) in zip(here, parts):
            o_ref[r] = _dot(p.astype(BF16), kv_ref[r, :, HEAD:]) / l
            lse_ref[r] = jnp.broadcast_to(high + jnp.log2(l), (GROUP, HEAD))


def _suffix(lengths, q, kv):
    rows, span = kv.shape[0], kv.shape[1]
    shape = jax.ShapeDtypeStruct((rows, GROUP, HEAD), F32)
    vmem = pl.BlockSpec(memory_space=pltpu.VMEM)
    return pl.pallas_call(
        _suffix_kernel,
        in_specs=[
            pl.BlockSpec(memory_space=pltpu.SMEM),
            vmem,
            pl.BlockSpec(memory_space=pltpu.HBM),
        ],
        out_specs=[vmem, vmem],
        out_shape=[shape, shape],
        scratch_shapes=[
            pltpu.VMEM(kv.shape, BF16),
            pltpu.SemaphoreType.DMA((8,)),
        ],
        compiler_params=_params(24, False),
        cost_estimate=pl.CostEstimate(
            flops=10**9, bytes_accessed=rows * span * 512, transcendentals=2**17
        ),
        name="suffix_attention",
    )(lengths, q.reshape(rows, GROUP, HEAD), _in_hbm(kv))


def _project_kernel(
    tenant_ref,
    recv_ref,
    o_ref,
    lse_ref,
    w_hbm,
    down_hbm,
    out_ref,
    att,
    low,
    w_ref,
    down_ref,
    sems,
):
    parts, rows = recv_ref.shape[0], recv_ref.shape[1]
    step = pl.program_id(0)
    width = w_ref.shape[2]

    def fetch_w(d):
        at = pl.multiple_of(d * width, HEAD)
        return pltpu.make_async_copy(
            w_hbm.at[:, pl.ds(at, width)], w_ref.at[d], sems.at[d]
        )

    fetch_down = pltpu.make_async_copy(down_hbm, down_ref, sems.at[w_ref.shape[0]])

    @pl.when(step == 0)
    def _():
        fetch_down.start()
        for d in range(w_ref.shape[0]):
            fetch_w(d).start()
        lane = _lane((rows, HEAD))
        own = jnp.zeros((rows, HEAD), F32)
        for g in range(GROUP):
            own = jnp.where(lane == g, lse_ref[:, g, :], own)
        lses = [own] + [
            _unpack3(recv_ref[w, :, GROUP * HEAD :].astype(F32)) for w in range(parts)
        ]
        top = functools.reduce(jnp.maximum, lses)
        weights = [jnp.exp2(x - top) for x in lses]
        z = functools.reduce(jnp.add, weights)
        weights = [x / z for x in weights]
        for g in range(GROUP):
            cols = slice(g * HEAD, (g + 1) * HEAD)
            acc = weights[0][:, g : g + 1] * o_ref[:, g, :]
            for w in range(parts):
                acc += weights[1 + w][:, g : g + 1] * recv_ref[w, :, cols].astype(F32)
            att[:, cols] = acc.astype(BF16)
        fetch_down.wait()
        reduced = _dot(att[...], down_ref[...])
        mine = _lane(reduced.shape) // RANK == tenant_ref[...]
        reduced = jnp.where(mine, reduced, 0.0)
        kept = reduced[:, :HEAD]
        for c in range(HEAD, reduced.shape[1], HEAD):
            kept = kept + reduced[:, c : c + HEAD]
        low[...] = kept.astype(BF16)

    fetch_w(step).wait()
    out_ref[0, :, :width] = _dot(att[...], w_ref[step]).astype(BF16)
    out_ref[0, :, width:] = low[...]


def _project(tenant, recv, o, lse, weight, down, parts):
    rows = recv.shape[1]
    depth, features = weight.shape
    width = features // parts

    def whole(shape):
        return pl.BlockSpec(shape, lambda d: (0,) * len(shape))

    return pl.pallas_call(
        _project_kernel,
        grid=(parts,),
        in_specs=[
            whole((rows, 1)),
            whole(recv.shape),
            whole(o.shape),
            whole(lse.shape),
            pl.BlockSpec(memory_space=pltpu.HBM),
            pl.BlockSpec(memory_space=pltpu.HBM),
        ],
        out_specs=pl.BlockSpec((1, rows, width + HEAD), lambda d: (d, 0, 0)),
        out_shape=jax.ShapeDtypeStruct((parts, rows, width + HEAD), BF16),
        scratch_shapes=[
            pltpu.VMEM((rows, GROUP * HEAD), BF16),
            pltpu.VMEM((rows, HEAD), BF16),
            pltpu.VMEM((parts, depth, width), BF16),
            pltpu.VMEM(down.shape, BF16),
            pltpu.SemaphoreType.DMA((parts + 1,)),
        ],
        compiler_params=_params(32),
        cost_estimate=pl.CostEstimate(
            flops=2 * rows * depth * features,
            bytes_accessed=2 * depth * features,
            transcendentals=0,
        ),
        name="project",
    )(tenant, recv, o, lse, _in_hbm(weight), _in_hbm(down))


def _finish_kernel(tenant_ref, recv_ref, up_ref, out_ref):
    parts, rows = recv_ref.shape[0], recv_ref.shape[1]
    width = out_ref.shape[1]
    total = recv_ref[0].astype(F32)
    for w in range(1, parts):
        total += recv_ref[w].astype(F32)
    depth = up_ref.shape[0]
    low = jnp.concatenate([total[:, width:]] * (depth // HEAD), axis=1)
    mine = _lane((rows, depth)) // RANK == tenant_ref[...]
    chosen = jnp.where(mine, low, 0.0).astype(BF16)
    out_ref[...] = (total[:, :width] + _dot(chosen, up_ref[...])).astype(BF16)


def _finish(tenant, recv, up):
    vmem = pl.BlockSpec(memory_space=pltpu.VMEM)
    return pl.pallas_call(
        _finish_kernel,
        in_specs=[vmem] * 3,
        out_specs=vmem,
        out_shape=jax.ShapeDtypeStruct((recv.shape[1], up.shape[1]), BF16),
        compiler_params=_params(16, False),
        name="finish",
    )(tenant, recv, up)


def per_device(
    queries,
    tenant,
    tenant_node_slot,
    suffix_length,
    system_prompt_cache,
    instruction_node_cache,
    suffix_cache,
    output_projection_weight,
    adapter_down_weight,
    adapter_up_weight,
):
    rows, width = queries.shape
    n_wide = lax.axis_size("wide")
    n_narrow = lax.axis_size("narrow")
    chips = n_wide // 2
    layers = chips // 2
    position = lax.axis_index("wide")
    layer, side, core = position // 4, position // 2 % 2, position % 2
    same_core = [[2 * j + c for j in range(chips)] for c in range(2)]
    sibling = [(i, i ^ 1) for i in range(n_wide)]
    n_slots = tenant_node_slot.shape[0]
    span = instruction_node_cache.shape[1]

    own = system_prompt_cache.reshape(-1, 2 * HEAD)
    sib = lax.ppermute(own, "wide", sibling)

    beside = lax.ppermute(queries, "wide", [(i, i ^ 2) for i in range(n_wide)])
    by_head = jnp.transpose(instruction_node_cache, (2, 0, 1, 3))
    place = jnp.stack([layer, core])
    beside, by_head, place = lax.optimization_barrier((beside, by_head, place))
    nodes = lax.all_to_all(by_head, "narrow", 0, 0, tiled=True)
    nodes = nodes.reshape(n_slots, span, 2 * HEAD)

    pair = jnp.where(
        side == 0,
        jnp.concatenate([queries, beside]),
        jnp.concatenate([beside, queries]),
    )
    pieces = [pair] + [
        lax.ppermute(pair, "wide", [((i + 4 * d) % n_wide, i) for i in range(n_wide)])
        for d in range(1, layers)
    ]
    keys, values = _keys(own, sib)
    o_a, lse_a = _system(pieces[:1], keys, values)
    *pieces[1:], lse_a[0] = lax.optimization_barrier((*pieces[1:], lse_a[0]))
    o_b, lse_b = _system(pieces[1:], keys, values)
    o_sys, lse_sys = [*o_a, *o_b], [*lse_a, *lse_b]
    nodes, lse_sys[-1], *pieces = lax.optimization_barrier(
        (nodes, lse_sys[-1], *pieces)
    )
    nodes_sib = lax.ppermute(nodes, "wide", sibling)
    qs, back, table = _plan(place, tenant_node_slot, tenant, pieces)

    o_suf, lse_suf = _suffix(
        suffix_length, queries, suffix_cache.reshape(rows, -1, 2 * HEAD)
    )
    sent = _node(table, place, qs, back, nodes, nodes_sib, o_sys, lse_sys)
    recv = lax.all_to_all(
        sent.reshape(chips, rows, -1),
        "wide",
        0,
        0,
        axis_index_groups=same_core,
        tiled=True,
    )
    my_tenant = lax.dynamic_slice_in_dim(tenant, position * rows, rows, 0)[:, None]
    parts = _project(
        my_tenant,
        recv,
        o_suf,
        lse_suf,
        output_projection_weight,
        adapter_down_weight,
        n_narrow,
    )
    parts = lax.all_to_all(parts, "narrow", 0, 0, tiled=True)
    return _finish(my_tenant, parts, adapter_up_weight)


def solution(mesh):
    return jax.shard_map(
        per_device,
        mesh=mesh,
        in_specs=(
            P("wide", "narrow"),
            P(),
            P(),
            P("wide"),
            P("wide", "narrow", None),
            P("narrow", "wide", None, None),
            P("wide", None, "narrow", None),
            P("narrow", None),
            P("narrow", None),
            P(None, "narrow"),
        ),
        out_specs=P("wide", "narrow"),
        check_vma=False,
    )
```

```python
import functools

import jax
import jax.numpy as jnp
from jax import lax
from jax.experimental import pallas as pl
from jax.experimental.pallas import tpu as pltpu
from jax.sharding import PartitionSpec as P

HEAD = 128
GROUP = 8
RANK = 16
F32 = jnp.float32
BF16 = jnp.bfloat16
SCALE2 = HEAD**-0.5 * 1.4426950408889634
FLOOR = -1e30
KEY_BLOCK = 512
ONES = 16
VISIT_ROWS = 16
VISIT_UNROLL = 16


def _params(mib, grid=True):
    return pltpu.CompilerParams(
        vmem_limit_bytes=mib << 20,
        dimension_semantics=("arbitrary",) if grid else None,
    )


def _in_hbm(x):
    return pltpu.with_memory_space_constraint(x, pltpu.HBM)


def _in_vmem(x):
    return pltpu.with_memory_space_constraint(x, pltpu.VMEM)


def _lane(shape):
    return lax.broadcasted_iota(jnp.int32, shape, len(shape) - 1)


def _dot(a, b):
    return jnp.dot(a, b, preferred_element_type=F32)


def _keys_kernel(own_ref, sib_ref, k_ref, vt_ref):
    n = own_ref.shape[0]
    for i, ref in enumerate((own_ref, sib_ref)):
        at = slice(i * n, (i + 1) * n)
        k_ref[at, :] = ref[:, :HEAD]
        vt_ref[:HEAD, at] = ref[:, HEAD:].T
    vt_ref[HEAD:, :] = jnp.ones((ONES, 2 * n), BF16)


def _keys(own, sib):
    n = 2 * own.shape[0]
    vmem = pl.BlockSpec(memory_space=pltpu.VMEM)
    return pl.pallas_call(
        _keys_kernel,
        in_specs=[vmem] * 2,
        out_specs=[vmem] * 2,
        out_shape=[
            pltpu.VMEM((n, HEAD), BF16),
            pltpu.VMEM((HEAD + ONES, n), BF16),
        ],
        compiler_params=_params(16, False),
        cost_estimate=pl.CostEstimate(
            flops=0, bytes_accessed=8 * n * HEAD, transcendentals=0
        ),
        name="keys",
    )(own, sib)


def _system_kernel(count, *refs):
    q_hbm, (k_ref, vt_ref) = refs[:count], refs[count : count + 2]
    o_hbm, lse_hbm = refs[count + 2 : 2 * count + 2], refs[2 * count + 2 : 3 * count + 2]
    q_buf, qt, o_buf, lse_buf, sems = refs[3 * count + 2 :]
    rows, keys = q_buf.shape[1], k_ref.shape[0]
    heads = [slice(g * HEAD, (g + 1) * HEAD) for g in range(GROUP)]
    across = [slice(g * rows, (g + 1) * rows) for g in range(GROUP)]
    first = [
        pltpu.make_async_copy(q_hbm[b], q_buf.at[b], sems.at[b, 0])
        for b in range(count)
    ]
    for copy in first:
        copy.start()
    for b in range(count):
        first[b].wait()
        for g in range(GROUP):
            qt[b, :, across[g]] = q_buf[b, :, heads[g]].T
    items = [(b, k) for b in range(count) for k in range(0, keys, KEY_BLOCK)]

    def score(item):
        b, k = item
        return _dot(k_ref[k : k + KEY_BLOCK, :], qt[b])

    last = []
    top = total = None
    ahead = score(items[0])
    for i, (b, k) in enumerate(items):
        s = ahead
        if i + 1 < len(items):
            ahead = score(items[i + 1])
        high = jnp.max(s, axis=0, keepdims=True) * SCALE2
        if k:
            high = jnp.maximum(high, top)
        p = jnp.exp2(s * SCALE2 - high).astype(BF16)
        r = _dot(vt_ref[:, k : k + KEY_BLOCK], p)
        total = total * jnp.exp2(top - high) + r if k else r
        top = high
        if k + KEY_BLOCK < keys:
            continue
        l = total[HEAD : HEAD + 1, :]
        o = total[:HEAD, :] / l
        lse = top + jnp.log2(l)
        for g in range(GROUP):
            o_buf[b, :, heads[g]] = o[:, across[g]].T
        lse = jnp.concatenate(
            [lse[:, across[g]] for g in range(GROUP)]
            + [jnp.zeros((HEAD - GROUP, rows), F32)],
            axis=0,
        )
        lse_buf[b] = lse.T
        for j, (src, dst) in enumerate([(o_buf, o_hbm), (lse_buf, lse_hbm)]):
            copy = pltpu.make_async_copy(src.at[b], dst[b], sems.at[b, 1 + j])
            copy.start()
            last.append(copy)
    for copy in last:
        copy.wait()


def _system(qs, k, vt):
    count, rows, keys = len(qs), qs[0].shape[0], k.shape[0]
    vmem = pl.BlockSpec(memory_space=pltpu.VMEM)
    hbm = pl.BlockSpec(memory_space=pltpu.HBM)
    outs = pl.pallas_call(
        functools.partial(_system_kernel, count),
        in_specs=[hbm] * count + [vmem] * 2,
        out_specs=[hbm] * (2 * count),
        out_shape=[pltpu.HBM((rows, GROUP * HEAD), F32)] * count
        + [pltpu.HBM((rows, HEAD), F32)] * count,
        scratch_shapes=[
            pltpu.VMEM((count, rows, GROUP * HEAD), BF16),
            pltpu.VMEM((count, HEAD, GROUP * rows), BF16),
            pltpu.VMEM((count, rows, GROUP * HEAD), F32),
            pltpu.VMEM((count, rows, HEAD), F32),
            pltpu.SemaphoreType.DMA((count, 3)),
        ],
        compiler_params=_params(40, False),
        cost_estimate=pl.CostEstimate(
            flops=6 * count * rows * GROUP * keys * HEAD,
            bytes_accessed=count * rows * 6 * GROUP * HEAD + 6 * keys * HEAD,
            transcendentals=count * rows * GROUP * keys,
        ),
        name="system_attention",
    )(*map(_in_hbm, qs), *map(_in_vmem, [k, vt]))
    return list(outs[:count]), list(outs[count:])


def _split3(x):
    hi = x.astype(BF16)
    rest = x - hi.astype(F32)
    mid = rest.astype(BF16)
    lo = (rest - mid.astype(F32)).astype(BF16)
    return hi.astype(F32), mid.astype(F32), lo.astype(F32)


def _pack3(x):
    lane = _lane(x.shape)
    hi, mid, lo = _split3(x)
    packed = jnp.where(lane < GROUP, hi, pltpu.roll(mid, GROUP, 1))
    packed = jnp.where(lane < 2 * GROUP, packed, pltpu.roll(lo, 2 * GROUP, 1))
    return jnp.where(lane < 3 * GROUP, packed, 0.0).astype(BF16)


def _unpack3(x):
    return x + (pltpu.roll(x, HEAD - GROUP, 1) + pltpu.roll(x, HEAD - 2 * GROUP, 1))


def _plan_kernel(place, slot_ref, tenant_ref, *refs):
    q_hbm, (qs_ref, back_ref, table_ref, q_buf, sems) = refs[:-5], refs[-5:]
    fetches = [
        pltpu.make_async_copy(ref, q_buf.at[i], sems.at[i])
        for i, ref in enumerate(q_hbm)
    ]
    for fetch in fetches:
        fetch.start()
    rows = qs_ref.shape[0]
    piece = q_buf.shape[1]
    tenants = slot_ref.shape[1]
    width = table_ref.shape[1]

    def iota(shape, dim):
        return lax.broadcasted_iota(jnp.int32, shape, dim)

    def count(where, axis):
        return jnp.sum(where.astype(jnp.int32), axis=axis, keepdims=True)

    chips, both = tenant_ref.shape
    layer, core = place[0], place[1]
    turned = pltpu.roll(tenant_ref[...], (chips - 2 * layer) % chips, 0)
    turned = pltpu.roll(turned, core * (both // 2), 1)
    spread = jnp.concatenate(
        [
            jnp.broadcast_to(turned[j : j + 1, :], (both // 2, both))
            for j in range(chips)
        ],
        axis=0,
    )
    own_lane = iota(spread.shape, 1) == iota(spread.shape, 0) % (both // 2)
    t_col = jnp.sum(jnp.where(own_lane, spread, 0), axis=1, keepdims=True)
    square = iota((rows, rows), 0) == iota((rows, rows), 1)
    t_row = jnp.sum(jnp.where(square, t_col, 0), axis=0, keepdims=True)
    square = iota((tenants, tenants), 0) == iota((tenants, tenants), 1)
    slot_col = jnp.sum(jnp.where(square, slot_ref[...], 0), axis=1, keepdims=True)

    key_row = t_row * rows + iota((1, rows), 1)
    key_col = t_col * rows + iota((rows, 1), 0)
    rank_row = count(key_col < key_row, 0)
    rank_col = count(key_row < key_col, 1)
    to_sorted = (iota((rows, rows), 0) == rank_row).astype(F32).astype(BF16)
    back_ref[...] = (iota((rows, rows), 1) == rank_col).astype(F32).astype(BF16)
    for fetch in fetches:
        fetch.wait()
    qs_ref[...] = sum(
        _dot(to_sorted[:, i * piece : (i + 1) * piece], q_buf[i])
        for i in range(len(fetches))
    ).astype(BF16)

    def visits_of(low, high):
        first = low // VISIT_ROWS
        last = (high + VISIT_ROWS - 1) // VISIT_ROWS
        return first, jnp.where(high > low, last - first, 0)

    lane = iota((1, width), 1)
    _, n_row = visits_of(count(t_col < lane, 0), count(t_col < lane + 1, 0))
    t = iota((tenants, 1), 0)
    low, high = count(t_row < t, 1), count(t_row < t + 1, 1)
    first, n = visits_of(low, high)
    start = jnp.sum(jnp.where(lane < t, n_row, 0), axis=1, keepdims=True)
    here = (lane >= start) & (lane < start + n)

    def pick(column):
        return jnp.sum(jnp.where(here, column, 0), axis=0, keepdims=True)

    table_ref[...] = jnp.concatenate(
        [
            pick(first - start + lane),
            pick(slot_col),
            pick(low),
            pick(high),
            jnp.broadcast_to(jnp.sum(n, axis=0, keepdims=True), (1, width)),
        ]
        + [jnp.zeros((1, width), jnp.int32)] * 3,
        axis=0,
    )


def _plan(place, slots, tenant, qs):
    rows, width = sum(q.shape[0] for q in qs), qs[0].shape[1]
    chips = 2 * len(qs)
    vmem = pl.BlockSpec(memory_space=pltpu.VMEM)
    return pl.pallas_call(
        _plan_kernel,
        in_specs=[pl.BlockSpec(memory_space=pltpu.SMEM)]
        + [vmem] * 2
        + [pl.BlockSpec(memory_space=pltpu.HBM)] * len(qs),
        out_specs=[vmem] * 3,
        out_shape=[
            pltpu.VMEM((rows, width), BF16),
            pltpu.VMEM((rows, rows), BF16),
            jax.ShapeDtypeStruct((8, HEAD), jnp.int32),
        ],
        scratch_shapes=[
            pltpu.VMEM((len(qs), *qs[0].shape), BF16),
            pltpu.SemaphoreType.DMA((len(qs),)),
        ],
        compiler_params=_params(16, False),
        cost_estimate=pl.CostEstimate(
            flops=2 * rows * rows * width,
            bytes_accessed=6 * rows * width,
            transcendentals=0,
        ),
        name="plan",
    )(place, slots[None, :], tenant.reshape(chips, -1), *map(_in_hbm, qs))


def _node_kernel(count, table, place, qs, back_ref, own_ref, sib_ref, *refs):
    o_hbm, lse_hbm = refs[:count], refs[count : 2 * count]
    out_ref, on, lse_n, o_buf, lse_buf, done, sems = refs[2 * count :]
    fetches = []
    for i in range(count):
        fetches += [
            pltpu.make_async_copy(o_hbm[i], o_buf.at[i], sems.at[i]),
            pltpu.make_async_copy(lse_hbm[i], lse_buf.at[i], sems.at[count + i]),
        ]
    for fetch in fetches:
        fetch.start()
    vr = VISIT_ROWS
    lane = _lane((vr, HEAD))
    row_in_block = lax.broadcasted_iota(jnp.int32, (vr, HEAD), 0)
    dims = (((1,), (1,)), ((), ()))

    def step(i, carry):
        blocks, spans, scores, slots = [], [], [], []
        for u in range(VISIT_UNROLL):
            v = i * VISIT_UNROLL + u
            at = pl.ds(pl.multiple_of(table[0, v] * vr, vr), vr)
            slot = table[1, v]
            qb = jnp.concatenate(
                [qs[at, g * HEAD : (g + 1) * HEAD] for g in range(GROUP)], axis=0
            )
            scores.append(
                [
                    lax.dot_general(
                        qb, ref[slot, :, :HEAD], dims, preferred_element_type=F32
                    )
                    for ref in (own_ref, sib_ref)
                ]
            )
            blocks.append(at)
            slots.append(slot)
            row = row_in_block + table[0, v] * vr
            spans.append((row >= table[2, v]) & (row < table[3, v]))
        tops, parts = [], []
        for s0, s1 in scores:
            high = jnp.max(jnp.maximum(s0, s1), axis=1, keepdims=True) * SCALE2
            p0 = jnp.exp2(s0 * SCALE2 - high)
            p1 = jnp.exp2(s1 * SCALE2 - high)
            tops.append(high)
            parts.append((p0, p1))
        results = []
        for (p0, p1), slot in zip(parts, slots):
            l = jnp.sum(p0 + p1, axis=1, keepdims=True)
            r = _dot(p0.astype(BF16), own_ref[slot, :, HEAD:]) + _dot(
                p1.astype(BF16), sib_ref[slot, :, HEAD:]
            )
            results.append((r, l))
        for at, inside, high, (r, l) in zip(blocks, spans, tops, results):
            o = r / l
            lse = high + jnp.log2(l)
            packed = jnp.zeros((vr, HEAD), F32)
            for g in range(GROUP):
                sub = slice(g * vr, (g + 1) * vr)
                cols = slice(g * HEAD, (g + 1) * HEAD)
                on[at, cols] = jnp.where(inside, o[sub, :], on[at, cols].astype(F32)).astype(
                    BF16
                )
                packed = jnp.where(lane == g, lse[sub, :], packed)
            lse_n[at, :] = jnp.where(inside, packed, lse_n[at, :])
        return carry

    lax.fori_loop(0, (table[4, 0] + VISIT_UNROLL - 1) // VISIT_UNROLL, step, 0)

    packed_lse = _pack3(lse_n[...])
    piece = done.shape[1]
    sends = []
    for i in range(count):
        back = back_ref[i * piece : (i + 1) * piece, :]
        lse_node = _unpack3(_dot(back, packed_lse))
        o_node = _dot(back, on[...])
        fetches[2 * i].wait()
        fetches[2 * i + 1].wait()
        lse_sys = lse_buf[i]
        top = jnp.maximum(lse_sys, lse_node)
        w_sys, w_node = jnp.exp2(lse_sys - top), jnp.exp2(lse_node - top)
        z = w_sys + w_node
        done[i, :, GROUP * HEAD :] = _pack3(top + jnp.log2(z))
        w_node = w_node / z
        for g in range(GROUP):
            cols = slice(g * HEAD, (g + 1) * HEAD)
            o_sys = o_buf[i, :, cols]
            o = o_sys + w_node[:, g : g + 1] * (o_node[:, cols] - o_sys)
            done[i, :, cols] = o.astype(BF16)
        layer = lax.rem(place[0] + i, count)
        to = pl.ds(pl.multiple_of(layer * piece, piece), piece)
        send = pltpu.make_async_copy(done.at[i], out_ref.at[to], sems.at[2 * count + i])
        send.start()
        sends.append(send)
    for send in sends:
        send.wait()


def _node(table, place, qs, back, own, sib, o_sys, lse_sys):
    rows, count = qs.shape[0], len(o_sys)
    smem = pl.BlockSpec(memory_space=pltpu.SMEM)
    hbm = pl.BlockSpec(memory_space=pltpu.HBM)
    piece = o_sys[0].shape[0]
    vmem = pl.BlockSpec(memory_space=pltpu.VMEM)
    return pl.pallas_call(
        functools.partial(_node_kernel, count),
        in_specs=[smem] * 2 + [vmem] * 4 + [hbm] * (2 * count),
        out_specs=hbm,
        out_shape=pltpu.HBM((rows, (GROUP + 1) * HEAD), BF16),
        scratch_shapes=[
            pltpu.VMEM((rows, GROUP * HEAD), BF16),
            pltpu.VMEM((rows, HEAD), F32),
            pltpu.VMEM((count, piece, GROUP * HEAD), F32),
            pltpu.VMEM((count, piece, HEAD), F32),
            pltpu.VMEM((count, piece, (GROUP + 1) * HEAD), BF16),
            pltpu.SemaphoreType.DMA((3 * count,)),
        ],
        compiler_params=_params(24, False),
        cost_estimate=pl.CostEstimate(
            flops=2 * 10**9, bytes_accessed=8 * 2**20, transcendentals=2**20
        ),
        name="node_attention",
    )(
        table,
        place,
        *map(_in_vmem, [qs, back, own, sib]),
        *map(_in_hbm, [*o_sys, *lse_sys]),
    )


def _suffix_kernel(len_ref, q_ref, kv_hbm, o_ref, lse_ref, kv_ref, sems):
    rows, span = kv_ref.shape[0], kv_ref.shape[1]
    block = rows // sems.shape[0]
    fetches = [
        pltpu.make_async_copy(
            kv_hbm.at[pl.ds(i * block, block)],
            kv_ref.at[pl.ds(i * block, block)],
            sems.at[i],
        )
        for i in range(sems.shape[0])
    ]
    for fetch in fetches:
        fetch.start()
    position = _lane((GROUP, span))
    dims = (((1,), (1,)), ((), ()))
    for i, fetch in enumerate(fetches):
        fetch.wait()
        here = range(i * block, (i + 1) * block)
        scores = [
            lax.dot_general(
                q_ref[r], kv_ref[r, :, :HEAD], dims, preferred_element_type=F32
            )
            for r in here
        ]
        parts = []
        for r, s in zip(here, scores):
            usable = position < len_ref[r]
            s = jnp.where(usable, s * SCALE2, FLOOR)
            high = jnp.max(s, axis=1, keepdims=True)
            p = jnp.where(usable, jnp.exp2(s - high), 0.0)
            parts.append((p, high, jnp.sum(p, axis=1, keepdims=True)))
        for r, (p, high, l) in zip(here, parts):
            o_ref[r] = _dot(p.astype(BF16), kv_ref[r, :, HEAD:]) / l
            lse_ref[r] = jnp.broadcast_to(high + jnp.log2(l), (GROUP, HEAD))


def _suffix(lengths, q, kv):
    rows, span = kv.shape[0], kv.shape[1]
    shape = jax.ShapeDtypeStruct((rows, GROUP, HEAD), F32)
    vmem = pl.BlockSpec(memory_space=pltpu.VMEM)
    return pl.pallas_call(
        _suffix_kernel,
        in_specs=[
            pl.BlockSpec(memory_space=pltpu.SMEM),
            vmem,
            pl.BlockSpec(memory_space=pltpu.HBM),
        ],
        out_specs=[vmem, vmem],
        out_shape=[shape, shape],
        scratch_shapes=[
            pltpu.VMEM(kv.shape, BF16),
            pltpu.SemaphoreType.DMA((8,)),
        ],
        compiler_params=_params(24, False),
        cost_estimate=pl.CostEstimate(
            flops=10**9, bytes_accessed=rows * span * 512, transcendentals=2**17
        ),
        name="suffix_attention",
    )(lengths, q.reshape(rows, GROUP, HEAD), _in_hbm(kv))


def _project_kernel(
    tenant_ref,
    recv_ref,
    o_ref,
    lse_ref,
    w_hbm,
    down_hbm,
    out_ref,
    att,
    low,
    w_ref,
    down_ref,
    sems,
):
    parts, rows = recv_ref.shape[0], recv_ref.shape[1]
    step = pl.program_id(0)
    width = w_ref.shape[2]

    def fetch_w(d):
        at = pl.multiple_of(d * width, HEAD)
        return pltpu.make_async_copy(
            w_hbm.at[:, pl.ds(at, width)], w_ref.at[d], sems.at[d]
        )

    fetch_down = pltpu.make_async_copy(down_hbm, down_ref, sems.at[w_ref.shape[0]])

    @pl.when(step == 0)
    def _():
        fetch_down.start()
        for d in range(w_ref.shape[0]):
            fetch_w(d).start()
        lane = _lane((rows, HEAD))
        own = jnp.zeros((rows, HEAD), F32)
        for g in range(GROUP):
            own = jnp.where(lane == g, lse_ref[:, g, :], own)
        lses = [own] + [
            _unpack3(recv_ref[w, :, GROUP * HEAD :].astype(F32)) for w in range(parts)
        ]
        top = functools.reduce(jnp.maximum, lses)
        weights = [jnp.exp2(x - top) for x in lses]
        z = functools.reduce(jnp.add, weights)
        weights = [x / z for x in weights]
        for g in range(GROUP):
            cols = slice(g * HEAD, (g + 1) * HEAD)
            acc = weights[0][:, g : g + 1] * o_ref[:, g, :]
            for w in range(parts):
                acc += weights[1 + w][:, g : g + 1] * recv_ref[w, :, cols].astype(F32)
            att[:, cols] = acc.astype(BF16)
        fetch_down.wait()
        reduced = _dot(att[...], down_ref[...])
        mine = _lane(reduced.shape) // RANK == tenant_ref[...]
        reduced = jnp.where(mine, reduced, 0.0)
        kept = reduced[:, :HEAD]
        for c in range(HEAD, reduced.shape[1], HEAD):
            kept = kept + reduced[:, c : c + HEAD]
        low[...] = kept.astype(BF16)

    for i in range(out_ref.shape[0]):
        d = step * out_ref.shape[0] + i
        fetch_w(d).wait()
        out_ref[i, :, :width] = _dot(att[...], w_ref[d]).astype(BF16)
        out_ref[i, :, width:] = low[...]


def _project(tenant, recv, o, lse, weight, down, parts):
    rows = recv.shape[1]
    depth, features = weight.shape
    width = features // parts

    def whole(shape):
        return pl.BlockSpec(shape, lambda d: (0,) * len(shape))

    return pl.pallas_call(
        _project_kernel,
        grid=(parts // 4,),
        in_specs=[
            whole((rows, 1)),
            whole(recv.shape),
            whole(o.shape),
            whole(lse.shape),
            pl.BlockSpec(memory_space=pltpu.HBM),
            pl.BlockSpec(memory_space=pltpu.HBM),
        ],
        out_specs=pl.BlockSpec((4, rows, width + HEAD), lambda d: (d, 0, 0)),
        out_shape=jax.ShapeDtypeStruct((parts, rows, width + HEAD), BF16),
        scratch_shapes=[
            pltpu.VMEM((rows, GROUP * HEAD), BF16),
            pltpu.VMEM((rows, HEAD), BF16),
            pltpu.VMEM((parts, depth, width), BF16),
            pltpu.VMEM(down.shape, BF16),
            pltpu.SemaphoreType.DMA((parts + 1,)),
        ],
        compiler_params=_params(32),
        cost_estimate=pl.CostEstimate(
            flops=2 * rows * depth * features,
            bytes_accessed=2 * depth * features,
            transcendentals=0,
        ),
        name="project",
    )(tenant, recv, o, lse, _in_hbm(weight), _in_hbm(down))


def _finish_kernel(tenant_ref, recv_ref, up_ref, out_ref):
    parts, rows = recv_ref.shape[0], recv_ref.shape[1]
    width = out_ref.shape[1]
    total = recv_ref[0].astype(F32)
    for w in range(1, parts):
        total += recv_ref[w].astype(F32)
    depth = up_ref.shape[0]
    low = jnp.concatenate([total[:, width:]] * (depth // HEAD), axis=1)
    mine = _lane((rows, depth)) // RANK == tenant_ref[...]
    chosen = jnp.where(mine, low, 0.0).astype(BF16)
    out_ref[...] = (total[:, :width] + _dot(chosen, up_ref[...])).astype(BF16)


def _finish(tenant, recv, up):
    vmem = pl.BlockSpec(memory_space=pltpu.VMEM)
    return pl.pallas_call(
        _finish_kernel,
        in_specs=[vmem] * 3,
        out_specs=vmem,
        out_shape=jax.ShapeDtypeStruct((recv.shape[1], up.shape[1]), BF16),
        compiler_params=_params(16, False),
        name="finish",
    )(tenant, recv, up)


def per_device(
    queries,
    tenant,
    tenant_node_slot,
    suffix_length,
    system_prompt_cache,
    instruction_node_cache,
    suffix_cache,
    output_projection_weight,
    adapter_down_weight,
    adapter_up_weight,
):
    rows, width = queries.shape
    n_wide = lax.axis_size("wide")
    n_narrow = lax.axis_size("narrow")
    chips = n_wide // 2
    layers = chips // 2
    position = lax.axis_index("wide")
    layer, side, core = position // 4, position // 2 % 2, position % 2
    same_core = [[2 * j + c for j in range(chips)] for c in range(2)]
    sibling = [(i, i ^ 1) for i in range(n_wide)]
    n_slots = tenant_node_slot.shape[0]
    span = instruction_node_cache.shape[1]

    own = system_prompt_cache.reshape(-1, 2 * HEAD)
    sib = lax.ppermute(own, "wide", sibling)

    beside = lax.ppermute(queries, "wide", [(i, i ^ 2) for i in range(n_wide)])
    by_head = jnp.transpose(instruction_node_cache, (2, 0, 1, 3))
    place = jnp.stack([layer, core])
    beside, by_head, place = lax.optimization_barrier((beside, by_head, place))
    nodes = lax.all_to_all(by_head, "narrow", 0, 0, tiled=True)
    nodes = nodes.reshape(n_slots, span, 2 * HEAD)

    pair = jnp.where(
        side == 0,
        jnp.concatenate([queries, beside]),
        jnp.concatenate([beside, queries]),
    )
    pieces = [pair] + [
        lax.ppermute(pair, "wide", [((i + 4 * d) % n_wide, i) for i in range(n_wide)])
        for d in range(1, layers)
    ]
    keys, values = _keys(own, sib)
    o_a, lse_a = _system(pieces[:1], keys, values)
    *pieces[1:], lse_a[0] = lax.optimization_barrier((*pieces[1:], lse_a[0]))
    o_b, lse_b = _system(pieces[1:], keys, values)
    o_sys, lse_sys = [*o_a, *o_b], [*lse_a, *lse_b]
    nodes, lse_sys[-1], *pieces = lax.optimization_barrier(
        (nodes, lse_sys[-1], *pieces)
    )
    nodes_sib = lax.ppermute(nodes, "wide", sibling)
    qs, back, table = _plan(place, tenant_node_slot, tenant, pieces)

    o_suf, lse_suf = _suffix(
        suffix_length, queries, suffix_cache.reshape(rows, -1, 2 * HEAD)
    )
    sent = _node(table, place, qs, back, nodes, nodes_sib, o_sys, lse_sys)
    recv = lax.all_to_all(
        sent.reshape(chips, rows, -1),
        "wide",
        0,
        0,
        axis_index_groups=same_core,
        tiled=True,
    )
    my_tenant = lax.dynamic_slice_in_dim(tenant, position * rows, rows, 0)[:, None]
    parts = _project(
        my_tenant,
        recv,
        o_suf,
        lse_suf,
        output_projection_weight,
        adapter_down_weight,
        n_narrow,
    )
    parts = lax.all_to_all(parts, "narrow", 0, 0, tiled=True)
    return _finish(my_tenant, parts, adapter_up_weight)


def solution(mesh):
    return jax.shard_map(
        per_device,
        mesh=mesh,
        in_specs=(
            P("wide", "narrow"),
            P(),
            P(),
            P("wide"),
            P("wide", "narrow", None),
            P("narrow", "wide", None, None),
            P("wide", None, "narrow", None),
            P("narrow", None),
            P("narrow", None),
            P(None, "narrow"),
        ),
        out_specs=P("wide", "narrow"),
        check_vma=False,
    )
```
